128 devices in a mesh: real: 8 (over y_lo, z), gen: 16 (over x, y_hi, core).
Axes of the slice: x: 4, y: 4 (y_hi: 2, y_lo: 2; y = y_hi * 2 + y_lo), z: 4, core: 2. Of those that a mesh axis runs over, the one named last changes fastest.
Arguments:
- hidden: float32 [4096, 256], P('gen'), may hold values from -6 to 6
- weight: float32 [256, 512], P(None, 'real'), may hold values from -0.375 to 0.375
- lengths: int32 [4096], P('gen'), may hold values from 1 to 512
- real_rows: float32 [131072, 256], P('real')
Outputs:
- update: float32 [256, 512], P(None, 'real')
- loss: float32 [], replicated
The draws below stay inside these ranges and needn't reach their ends.
All inputs are finite; a program needn't handle non-finite values.
Results may differ from the reference program's by a relative error of at most 0.0003.
Values sent between devices are 32-bit elements; how exact they have to be, the bound alone decides.
No kernel may reach another device: no remote copies, remote signals or barrier semaphores. Data moves between devices by JAX's collectives and lax.ppermute only.
A program may use at most 128 MiB of HBM per device.

```python
import math
import jax
import jax.numpy as jnp
from jax import lax

NUM_BINS = 256
SEQ_STEPS = 512
HID_WIDTH = 256
FLOW_TOTAL = 4096
REAL_TOTAL = 131072


def draw_lengths(key, part):
    key = jax.random.fold_in(key, 7)
    drawn = jax.random.randint(key, (FLOW_TOTAL,), 1, SEQ_STEPS + 1, dtype=jnp.int32)
    drawn = drawn.at[0].set(SEQ_STEPS)
    return drawn.at[FLOW_TOTAL - 1].set(1)


def bump_sum(centers, middle, sigma, spacing):
    width = jnp.sqrt(sigma * sigma + spacing * spacing)
    offset = centers[None, :] - middle
    return jnp.exp(-offset * offset / (2.0 * width * width)) / width


def draw_real_rows(key, part):
    key = jax.random.fold_in(key, 11)
    keys = jax.random.split(key, 7)
    spacing = 6.0 / NUM_BINS
    centers = (jnp.arange(NUM_BINS, dtype=jnp.float32) + 0.5) * spacing
    components = 3
    rough_lo, rough_hi, mass_lo, mass_hi = (0.7, 1.3, 0.5, 2.0)
    middles = jnp.exp(jax.random.uniform(keys[0], (REAL_TOTAL, components), jnp.float32, math.log(0.15), math.log(3.0)))
    sigmas = jnp.exp(jax.random.uniform(keys[1], (REAL_TOTAL, components), jnp.float32, math.log(0.08), math.log(0.8)))
    shares = jax.random.uniform(keys[2], (REAL_TOTAL, components), jnp.float32, 0.2, 1.0)
    shares = shares / (shares[:, 0:1] + shares[:, 1:2] + shares[:, 2:3])
    density = jnp.zeros((REAL_TOTAL, NUM_BINS), jnp.float32)
    for comp in range(components):
        density = density + shares[:, comp:comp + 1] * bump_sum(centers, middles[:, comp:comp + 1], sigmas[:, comp:comp + 1], spacing)
    rough = jax.random.uniform(keys[5], (REAL_TOTAL, NUM_BINS), jnp.float32, rough_lo, rough_hi)
    mass = jnp.exp(jax.random.uniform(keys[6], (REAL_TOTAL, 1), jnp.float32, math.log(mass_lo), math.log(mass_hi)))
    return (spacing * density * rough * mass).astype(jnp.float32)


def level_of(own_key, shape, shards, smallest, top_value):
    loudness, own = 1.0, jax.random.fold_in(own_key, 6)
    for axis_at, parts in shards:
        heights = jnp.exp(jax.random.uniform(jax.random.fold_in(own, axis_at), (parts,), jnp.float32, smallest / len(shards), top_value / len(shards)))
        loudness = loudness * jnp.repeat(heights, shape[axis_at] // parts).reshape([-1 if axis == axis_at else 1 for axis in range(len(shape))])
    return loudness


def normal_values(own_key, dims, scale, limit, cuts=(), kind=jnp.bfloat16):
    entries = scale * jax.random.normal(own_key, dims, jnp.float32)
    if cuts:
        entries = entries * level_of(own_key, dims, cuts, -0.22, 0.18)
    return jnp.clip(entries, -limit, limit).astype(kind)


def setup_inputs(seed: int = 0) -> dict:
    key_of = jax.random.split(jax.random.key(seed), 5)
    return {
        "hidden": normal_values(key_of[0], (FLOW_TOTAL, HID_WIDTH), 1.0, 6.0, ((0, 16),), jnp.float32),
        "weight": normal_values(key_of[1], (HID_WIDTH, SEQ_STEPS), HID_WIDTH ** -0.5, 0.375, ((1, 8),), jnp.float32),
        "lengths": draw_lengths(jax.random.fold_in(key_of[4], 71), 0),
        "real_rows": draw_real_rows(jax.random.fold_in(key_of[4], 71), 0),
    }


highest = lax.Precision.HIGHEST
scale_factors = (0.25, 0.5, 1.0, 2.0, 4.0)

def bin_table():
    spacing = 6.0 / NUM_BINS
    centers = (jnp.arange(NUM_BINS, dtype=jnp.float32) + 0.5) * spacing
    return (centers, spacing)

def pair_terms(left, left_sq, right, spread):
    inner_prod = jnp.einsum('ib,jb->ij', left, right, precision=highest)
    right_sq = lax.optimization_barrier(jnp.sum(right * right, 1))
    distance = left_sq[:, None] + right_sq[None, :] - 2.0 * inner_prod
    kernel = jnp.zeros_like(distance)
    weights = jnp.zeros_like(distance)
    for factor in scale_factors:
        kernel_width = factor * spread
        decayed = jnp.exp(-distance / kernel_width)
        kernel = kernel + decayed
        weights = weights + decayed / kernel_width
    return (jnp.sum(kernel), lax.optimization_barrier(jnp.sum(weights, 1)), jnp.dot(weights, right, precision=highest))

def reference(hidden, weight, lengths, real_rows):
    centers, spacing = bin_table()
    total_flows = hidden.shape[0]
    total_real = real_rows.shape[0]
    pre = jnp.dot(hidden, weight, precision=highest)
    values = jax.nn.softplus(pre)
    positions = jnp.arange(SEQ_STEPS, dtype=jnp.int32)
    mask = (positions[None, :] < lengths[:, None]).astype(jnp.float32)
    length_f = lengths.astype(jnp.float32)
    row_block = math.gcd(total_flows, 64)

    def hist_block(pieces):
        vals, masks = pieces
        offset = vals[:, :, None] - centers
        bumps = jnp.exp(-offset * offset / (2.0 * spacing * spacing))
        return jnp.einsum('gt,gtb->gb', masks, bumps, precision=highest)
    counts = lax.map(hist_block, (values.reshape(-1, row_block, SEQ_STEPS), mask.reshape(-1, row_block, SEQ_STEPS)))
    hist = counts.reshape(total_flows, NUM_BINS) / length_f[:, None]
    gen_sq = jnp.sum(hist * hist)
    gen_sum = lax.optimization_barrier(jnp.sum(hist, 0))
    real_sq = jnp.sum(real_rows * real_rows)
    real_sum = lax.optimization_barrier(jnp.sum(real_rows, 0))
    spread = gen_sq / total_flows + real_sq / total_real - 2.0 * jnp.dot(gen_sum / total_flows, real_sum / total_real, precision=highest)
    hist_sq = lax.optimization_barrier(jnp.sum(hist * hist, 1))
    block_rows = min(total_real, 2048)
    stacked = real_rows.reshape(-1, block_rows, NUM_BINS)

    def cross_step(carry, rows):
        part_k, part_row, part_mat = pair_terms(hist, hist_sq, rows, spread)
        return ((carry[0] + part_k, carry[1] + part_row, carry[2] + part_mat), None)
    start = (jnp.zeros((), jnp.float32), jnp.zeros((total_flows,), jnp.float32), jnp.zeros((total_flows, NUM_BINS), jnp.float32))
    (cross_k, cross_row, cross_mat), _ = lax.scan(cross_step, start, stacked)
    pair_k, pair_row, pair_mat = pair_terms(hist, hist_sq, hist, spread)
    loss = pair_k / (total_flows * total_flows) - 2.0 * cross_k / (total_flows * total_real)
    grad_hist = -4.0 / total_flows * (pair_row[:, None] * hist - pair_mat) + 4.0 / total_real * (cross_row[:, None] * hist - cross_mat)
    grad_counts = grad_hist / length_f[:, None]

    def back_block(pieces):
        vals, masks, grads = pieces
        offset = vals[:, :, None] - centers
        bumps = jnp.exp(-offset * offset / (2.0 * spacing * spacing))
        slope = jnp.einsum('gtb,gb->gt', bumps * -offset, grads, precision=highest)
        return masks * slope / (spacing * spacing)
    grad_steps = lax.map(back_block, (values.reshape(-1, row_block, SEQ_STEPS), mask.reshape(-1, row_block, SEQ_STEPS), grad_counts.reshape(-1, row_block, NUM_BINS)))
    grad_pre = grad_steps.reshape(total_flows, SEQ_STEPS) * jax.nn.sigmoid(pre)
    grad_weight = jnp.einsum('gz,gt->zt', hidden, grad_pre, precision=highest)
    mean_sq = jnp.sum(grad_weight * grad_weight) / (HID_WIDTH * SEQ_STEPS)
    update = grad_weight / jnp.sqrt(mean_sq + 1e-06)
    return (update, loss)
```

```python
import functools
import math

import jax
import jax.numpy as jnp
from jax import lax
from jax.experimental import pallas as pl
from jax.experimental.pallas import tpu as pltpu
from jax.sharding import PartitionSpec as P

NUM_BINS = 256
SEQ_STEPS = 512
HID_WIDTH = 256
SPACING = 6.0 / NUM_BINS
LOG2E = math.log2(math.e)
UNIT = math.sqrt(LOG2E / 2.0) / SPACING
STEP = UNIT * SPACING
FAR = 1.0e6

highest = lax.Precision.HIGHEST
f32 = jnp.float32
bf16 = jnp.bfloat16
NT = (((1,), (1,)), ((), ()))
NN = (((1,), (0,)), ((), ()))
VMEM = pltpu.VMEM
SMEM = pltpu.SMEM


def params(limit=48 << 20):
    return pltpu.CompilerParams(vmem_limit_bytes=limit)


def whole(space=VMEM):
    return pl.BlockSpec(memory_space=space)


def split(x):
    hi = x.astype(bf16)
    return hi, (x - hi.astype(f32)).astype(bf16)


def dot(a, b, dims):
    return lax.dot_general(a, b, dims, preferred_element_type=f32)


def count_kernel(first_ref, wt_ref, hid_ref, len_ref, out_ref, val_ref, sig_ref):
    pre = lax.dot_general(
        wt_ref[...], hid_ref[...], NT, precision=highest, preferred_element_type=f32
    )
    small = jnp.exp(-jnp.abs(pre))
    steps = jnp.maximum(pre, 0.0) + jnp.log1p(small)
    at = first_ref[0] + lax.broadcasted_iota(jnp.int32, pre.shape, 0)
    lens = len_ref[...]
    val = jnp.where(at < lens, steps * UNIT, FAR)
    val_ref[...] = val
    sig = 1.0 / (1.0 + jnp.exp(-pre))
    sig_ref[...] = sig / (lens.astype(f32) * (UNIT * SPACING * SPACING))
    tall, wide = val.shape

    @pl.loop(0, NUM_BINS // 8)
    def _(i):
        base = (8 * i).astype(f32) + 0.5
        rows = []
        for j in range(8):
            off = (base + j) * STEP - val
            e = jnp.exp2(-(off * off))
            rows.append(jnp.sum(e, 0, keepdims=True))
        out_ref[pl.ds(pl.multiple_of(8 * i, 8), 8), :] = jnp.concatenate(rows, 0)


def count_steps(first, wt, hidden, lens):
    t, g = wt.shape[0], hidden.shape[0]
    return pl.pallas_call(
        count_kernel,
        out_shape=[
            jax.ShapeDtypeStruct((NUM_BINS, g), f32),
            jax.ShapeDtypeStruct((t, g), f32),
            jax.ShapeDtypeStruct((t, g), f32),
        ],
        in_specs=[whole(SMEM), whole(), whole(), whole()],
        out_specs=[whole(), whole(), whole()],
        compiler_params=params(),
    )(first, wt, hidden, lens)


def back_kernel(gh_ref, val_ref, sig_ref, hid_ref, out_ref):
    val = val_ref[...]

    def bins(i, acc):
        base = (8 * i).astype(f32) + 0.5
        rows = gh_ref[pl.ds(pl.multiple_of(8 * i, 8), 8), :]
        for j in range(8):
            off = (base + j) * STEP - val
            e = jnp.exp2(-(off * off))
            acc = acc + (e * off) * rows[j : j + 1, :]
        return acc

    slope = lax.fori_loop(0, NUM_BINS // 8, bins, jnp.zeros_like(val))
    out_ref[...] = lax.dot_general(
        slope * sig_ref[...], hid_ref[...], NN, precision=highest, preferred_element_type=f32
    )


def back_steps(gh, val, sig, hidden):
    return pl.pallas_call(
        back_kernel,
        out_shape=jax.ShapeDtypeStruct((val.shape[0], hidden.shape[1]), f32),
        in_specs=[whole()] * 4,
        out_specs=whole(),
        compiler_params=params(),
    )(gh, val, sig, hidden)


def stat_kernel(rows_ref, sum_ref, sq_ref):
    rows = rows_ref[...]
    hi, lo = split(rows * rows)
    ones = jnp.ones((8, rows.shape[1]), bf16)
    sq_ref[...] = dot(ones, hi, NT) + dot(ones, lo, NT)
    part = jnp.sum(rows.reshape(-1, 8, rows.shape[1]), 0)

    @pl.when(pl.program_id(0) == 0)
    def _():
        sum_ref[...] = part

    @pl.when(pl.program_id(0) > 0)
    def _():
        sum_ref[...] += part


def row_stats(rows, block):
    n, w = rows.shape
    block = min(block, n)
    return pl.pallas_call(
        stat_kernel,
        grid=(n // block,),
        out_shape=[
            jax.ShapeDtypeStruct((8, w), f32),
            jax.ShapeDtypeStruct((8, n), f32),
        ],
        in_specs=[pl.BlockSpec((block, w), lambda i: (i, 0))],
        out_specs=[
            pl.BlockSpec((8, w), lambda i: (0, 0)),
            pl.BlockSpec((8, block), lambda i: (0, i)),
        ],
        compiler_params=params(),
    )(rows)


def pair_kernel(
    cols, rate_ref, ht_ref, rows_ref, sq_ref, out_ref, ker_ref,
    hh_ref, hl_ref, hs_ref, ip_ref, wh_ref, wl_ref, mat_ref, sum_ref, kacc_ref,
):
    flows = ht_ref.shape[1]
    rate = rate_ref[0]

    @pl.when(pl.program_id(0) == 0)
    def _():
        h = ht_ref[...].T
        hh, hl = split(h * (2.0 * rate))
        hh_ref[...] = hh
        hl_ref[...] = hl
        hs_ref[...] = jnp.broadcast_to(
            jnp.sum(h * h, 1, keepdims=True) * rate, hs_ref.shape
        )
        mat_ref[...] = jnp.zeros_like(mat_ref)
        sum_ref[...] = jnp.zeros_like(sum_ref)
        kacc_ref[...] = jnp.zeros_like(kacc_ref)

    parts = rows_ref.shape[0] // cols
    kacc = kacc_ref[...]
    for p in range(parts):
        rh, rl = split(rows_ref[p * cols : (p + 1) * cols, :])
        hh = hh_ref[...]
        slot = p % 2
        ip_ref[slot] = dot(hh, rh, NT) + dot(hl_ref[...], rh, NT) + dot(hh, rl, NT)
        sq = sq_ref[0:1, p * cols : (p + 1) * cols] * rate
        for c in range(flows // 16):
            at = slice(16 * c, 16 * c + 16)
            x = ip_ref[slot, at, :] - sq - jnp.tile(hs_ref[at, :], (1, cols // 128))
            u = jnp.exp2(x)
            u2 = u * u
            u4 = u2 * u2
            u8 = u4 * u4
            u16 = u8 * u8
            w = u16 + u16 + u8
            w = w + w + u4
            w = w + w + u2
            w = w + w + u
            k = ((u16 + u8) + (u4 + u2)) + u
            wh = w.astype(bf16)
            wh_ref[slot, at, :] = wh
            wl_ref[slot, at, :] = (w - wh.astype(f32)).astype(bf16)
            ws = w[:, 0:128]
            ks = k[:, 0:128]
            for q in range(1, cols // 128):
                ws = ws + w[:, 128 * q : 128 * q + 128]
                ks = ks + k[:, 128 * q : 128 * q + 128]
            sum_ref[at, :] += ws
            kacc = kacc + ks
        wh = wh_ref[slot]
        mat_ref[...] += dot(wh, rh, NN) + dot(wl_ref[slot], rh, NN) + dot(wh, rl, NN)
    kacc_ref[...] = kacc

    @pl.when(pl.program_id(0) == pl.num_programs(0) - 1)
    def _():
        h = ht_ref[...].T
        total = jnp.sum(sum_ref[...], 1, keepdims=True)
        out_ref[...] = ((total * h - mat_ref[...]) * rate).T
        ker_ref[...] = kacc_ref[...]


def pair_sums(rate, ht, rows, sq, block, cols):
    n, w = rows.shape
    flows = ht.shape[1]
    block = min(block, n)
    return pl.pallas_call(
        functools.partial(pair_kernel, cols),
        grid=(n // block,),
        out_shape=[
            jax.ShapeDtypeStruct((w, flows), f32),
            jax.ShapeDtypeStruct((16, 128), f32),
        ],
        in_specs=[
            whole(SMEM),
            pl.BlockSpec((w, flows), lambda i: (0, 0)),
            pl.BlockSpec((block, w), lambda i: (i, 0)),
            pl.BlockSpec((8, block), lambda i: (0, i)),
        ],
        out_specs=[
            pl.BlockSpec((w, flows), lambda i: (0, 0)),
            pl.BlockSpec((16, 128), lambda i: (0, 0)),
        ],
        scratch_shapes=[
            VMEM((flows, w), bf16),
            VMEM((flows, w), bf16),
            VMEM((flows, 128), f32),
            VMEM((2, flows, cols), f32),
            VMEM((2, flows, cols), bf16),
            VMEM((2, flows, cols), bf16),
            VMEM((flows, w), f32),
            VMEM((flows, 128), f32),
            VMEM((16, 128), f32),
        ],
        compiler_params=params(),
        cost_estimate=pl.CostEstimate(
            flops=4 * n * w * flows * 3,
            bytes_accessed=4 * n * w,
            transcendentals=n * flows,
        ),
    )(rate, ht, rows, sq)


def swap_sum(x, axis, count):
    hop = 1
    while hop < count:
        x = x + lax.ppermute(x, axis, [(i, i ^ hop) for i in range(count)])
        hop *= 2
    return x


def block_sum(x, axis, count):
    parts = x.reshape(count, x.shape[0] // count, x.shape[1])
    own = jnp.sum(lax.all_to_all(parts, axis, 0, 0, tiled=True), 0)
    every = lax.all_to_all(
        jnp.broadcast_to(own[None], parts.shape), axis, 0, 0, tiled=True
    )
    return every.reshape(x.shape)


def per_device(real_count, gen_count, hidden, weight, lengths, real_rows):
    real_index = lax.axis_index("real")
    flows = hidden.shape[0]
    local_steps = weight.shape[1]
    total_flows = flows * gen_count
    total_real = real_rows.shape[0] * real_count
    lens = lengths[None, :]
    first = jnp.full((1,), real_index * local_steps, jnp.int32)
    part_counts, val, sig = count_steps(first, weight.T, hidden, lens)
    real_sum, real_sq = row_stats(real_rows, 2048)
    real_vec = jnp.concatenate(
        [jnp.sum(real_sum, 0), jnp.full((128,), jnp.sum(real_sq[0]))]
    )[None, :]
    counts = block_sum(part_counts, "real", real_count)
    real_vec = swap_sum(real_vec, "real", real_count)
    hist_t = counts / lens.astype(f32)
    gen_vec = jnp.concatenate(
        [jnp.sum(hist_t, 1), jnp.full((128,), jnp.sum(hist_t * hist_t))]
    )[None, :]
    gen_vec = swap_sum(gen_vec, "gen", gen_count)
    spread = (
        gen_vec[0, NUM_BINS] / total_flows
        + real_vec[0, NUM_BINS] / total_real
        - 2.0
        * jnp.sum(
            (gen_vec[0, :NUM_BINS] / total_flows) * (real_vec[0, :NUM_BINS] / total_real)
        )
    )
    share = flows // real_count
    own = lax.dynamic_slice_in_dim(hist_t, real_index * share, share, 1).T
    others = lax.all_gather(own, "gen", axis=0, tiled=True)
    rate = (LOG2E / (4.0 * spread)).reshape(1)
    cross_g, cross_k = pair_sums(rate, hist_t, real_rows, real_sq, 1024, 256)
    _, other_sq = row_stats(others, 512)
    pair_g, pair_k = pair_sums(rate, hist_t, others, other_sq, 512, 256)
    grad_part = (cross_g * (4.0 / total_real) - pair_g * (4.0 / total_flows)) * (1.0 / LOG2E)
    loss_part = jnp.sum(pair_k) / (total_flows * total_flows) - 2.0 * jnp.sum(
        cross_k
    ) / (total_flows * total_real)
    grad_hist = block_sum(grad_part, "real", real_count)
    part = back_steps(grad_hist, val, sig, hidden)
    grad_weight = swap_sum(part, "gen", gen_count)
    loss_vec = swap_sum(jnp.full((1, 128), loss_part), "gen", gen_count)
    tail = jnp.concatenate(
        [jnp.full((1, 128), jnp.sum(grad_weight * grad_weight)), loss_vec], 1
    )
    tail = swap_sum(tail, "real", real_count)
    mean_sq = tail[0, 0] / (HID_WIDTH * SEQ_STEPS)
    update = grad_weight / jnp.sqrt(mean_sq + 1e-06)
    return (update.T, tail[0, 128])


def solution(mesh):
    in_specs = (P("gen", None), P(None, "real"), P("gen"), P("real", None))
    out_specs = (P(None, "real"), P())
    body = functools.partial(per_device, mesh.shape["real"], mesh.shape["gen"])
    return jax.shard_map(
        body, mesh=mesh, in_specs=in_specs, out_specs=out_specs, check_vma=False
    )
```

```python
import functools
import math

import jax
import jax.numpy as jnp
from jax import lax
from jax.experimental import pallas as pl
from jax.experimental.pallas import tpu as pltpu
from jax.sharding import PartitionSpec as P

NUM_BINS = 256
SEQ_STEPS = 512
HID_WIDTH = 256
SPACING = 6.0 / NUM_BINS
LOG2E = math.log2(math.e)
UNIT = math.sqrt(LOG2E / 2.0) / SPACING
STEP = UNIT * SPACING
FAR = 1.0e6
EXTRA = 8

highest = lax.Precision.HIGHEST
f32 = jnp.float32
bf16 = jnp.bfloat16
NT = (((1,), (1,)), ((), ()))
NN = (((1,), (0,)), ((), ()))
VMEM = pltpu.VMEM
SMEM = pltpu.SMEM


def params(limit=48 << 20):
    return pltpu.CompilerParams(vmem_limit_bytes=limit)


def fixed(shape):
    return pl.BlockSpec(shape, lambda i: (0,) * len(shape))


def call_once(kernel, outs, *args, scalars=0):
    return pl.pallas_call(
        kernel,
        grid=(1,),
        out_shape=[jax.ShapeDtypeStruct(s, f32) for s in outs],
        in_specs=[
            pl.BlockSpec(memory_space=SMEM) if i < scalars else fixed(a.shape)
            for i, a in enumerate(args)
        ],
        out_specs=[fixed(s) for s in outs],
        compiler_params=params(),
    )(*args)


def split(x):
    hi = x.astype(bf16)
    return hi, (x - hi.astype(f32)).astype(bf16)


def dot(a, b, dims):
    return lax.dot_general(a, b, dims, preferred_element_type=f32)


def count_kernel(first_ref, wt_ref, hid_ref, len_ref, out_ref, val_ref, sig_ref):
    pre = lax.dot_general(
        wt_ref[...], hid_ref[...], NT, precision=highest, preferred_element_type=f32
    )
    small = jnp.exp(-jnp.abs(pre))
    steps = jnp.maximum(pre, 0.0) + jnp.log1p(small)
    at = first_ref[0] + lax.broadcasted_iota(jnp.int32, pre.shape, 0)
    lens = len_ref[...]
    val = jnp.where(at < lens, steps * UNIT, FAR)
    val_ref[...] = val
    sig = 1.0 / (1.0 + jnp.exp(-pre))
    sig_ref[...] = sig / (lens.astype(f32) * (UNIT * SPACING * SPACING))

    def bins(i, carry):
        base = (8 * i).astype(f32) + 0.5
        rows = []
        for j in range(8):
            off = (base + j) * STEP - val
            e = jnp.exp2(-(off * off))
            rows.append(jnp.sum(e, 0, keepdims=True))
        out_ref[pl.ds(pl.multiple_of(8 * i, 8), 8), :] = jnp.concatenate(rows, 0)
        return carry

    lax.fori_loop(0, NUM_BINS // 8, bins, 0)
    out_ref[...] = out_ref[...].T


def back_kernel(gh_ref, val_ref, sig_ref, hid_ref, out_ref, ght_ref):
    parts, share = gh_ref.shape[0], gh_ref.shape[1] - EXTRA
    tall = val_ref.shape[0]
    gh = jnp.concatenate([gh_ref[p, :share, :] for p in range(parts)], 0)
    ght_ref[...] = gh.T
    val = val_ref[...]

    def bins(i, acc):
        base = (8 * i).astype(f32) + 0.5
        rows = ght_ref[pl.ds(pl.multiple_of(8 * i, 8), 8), :]
        for j in range(8):
            off = (base + j) * STEP - val
            e = jnp.exp2(-(off * off))
            acc = acc + (e * off) * rows[j : j + 1, :]
        return acc

    slope = lax.fori_loop(0, NUM_BINS // 8, bins, jnp.zeros_like(val))
    out_ref[0:tall, :] = lax.dot_general(
        slope * sig_ref[...], hid_ref[...], NN, precision=highest, preferred_element_type=f32
    )
    out_ref[tall:, :] = gh_ref[0, share:, :]


def back_steps(gh, val, sig, hidden):
    t, g = val.shape
    z = hidden.shape[1]
    return pl.pallas_call(
        back_kernel,
        grid=(1,),
        out_shape=jax.ShapeDtypeStruct((t + EXTRA, z), f32),
        in_specs=[fixed(gh.shape), fixed((t, g)), fixed((t, g)), fixed((g, z))],
        out_specs=fixed((t + EXTRA, z)),
        scratch_shapes=[VMEM((NUM_BINS, g), f32)],
        compiler_params=params(),
    )(gh, val, sig, hidden)


def row_squares(rows):
    hi, lo = split(rows * rows)
    ones = jnp.ones((8, 2 * rows.shape[1]), bf16)
    return dot(ones, jnp.concatenate([hi, lo], 1), NT)


def stat_kernel(rows_ref, sum_ref, near_ref, sq_ref):
    rows = rows_ref[...]
    near = rows.astype(bf16)
    near_ref[...] = near
    sq_ref[...] = row_squares(near.astype(f32))
    w = rows.shape[1]
    part = jnp.concatenate(
        [
            jnp.sum(rows.reshape(-1, 8, w), 0),
            jnp.sum((rows * rows).reshape(-1, 8, w), 0),
        ],
        0,
    )

    @pl.when(pl.program_id(0) == 0)
    def _():
        sum_ref[...] = part

    @pl.when(pl.program_id(0) > 0)
    def _():
        sum_ref[...] += part


def row_stats(rows, block):
    n, w = rows.shape
    block = min(block, n)
    return pl.pallas_call(
        stat_kernel,
        grid=(n // block,),
        out_shape=[
            jax.ShapeDtypeStruct((16, w), f32),
            jax.ShapeDtypeStruct((n, w), bf16),
            jax.ShapeDtypeStruct((8, n), f32),
        ],
        in_specs=[pl.BlockSpec((block, w), lambda i: (i, 0))],
        out_specs=[
            fixed((16, w)),
            pl.BlockSpec((block, w), lambda i: (i, 0)),
            pl.BlockSpec((8, block), lambda i: (0, i)),
        ],
        compiler_params=params(),
        cost_estimate=pl.CostEstimate(
            flops=32 * n * w, bytes_accessed=6 * n * w, transcendentals=0
        ),
    )(rows)


def share_kernel(parts_ref, len_ref, out_ref):
    count = jnp.sum(parts_ref[...], 0)
    hist = count / len_ref[...].astype(f32)
    out_ref[...] = jnp.broadcast_to(hist[None], out_ref.shape)


def load_kernel(others_ref, own_ref, real_ref, out_ref):
    parts, share, w = others_ref.shape
    rows = others_ref[...].reshape(parts * share, w)
    stats = jnp.concatenate(
        [
            jnp.sum(rows, 0, keepdims=True),
            jnp.sum(rows * rows, 0, keepdims=True),
            jnp.sum(real_ref[0:8, :], 0, keepdims=True),
            jnp.sum(real_ref[8:16, :], 0, keepdims=True),
            jnp.zeros((EXTRA - 4, w), f32),
        ],
        0,
    )
    load = jnp.concatenate([own_ref[0], stats], 0)
    out_ref[...] = jnp.broadcast_to(load[None], out_ref.shape)


def pair_kernel(
    cols, total_flows, total_real, hall_ref, others_ref, near_ref, sq_ref, out_ref,
    rate_ref, h_ref, hc_ref, hs_ref, ip_ref, wh_ref, mat_ref, sum_ref, kacc_ref,
):
    parts, tall, width = hall_ref.shape
    share = tall - EXTRA
    flows = parts * share

    @pl.when(pl.program_id(0) == 0)
    def _():
        h = jnp.concatenate([hall_ref[p, :share, :] for p in range(parts)], 0)
        h_ref[...] = h
        stats = hall_ref[0, share:, :]
        for p in range(1, parts):
            stats = stats + hall_ref[p, share:, :]
        line = (
            stats[1:2, :] / total_flows
            + stats[3:4, :] / total_real
            - 2.0 * ((stats[0:1, :] / total_flows) * (stats[2:3, :] / total_real))
        )
        spread = jnp.sum(line, 1, keepdims=True)
        rate = jnp.broadcast_to(LOG2E / (4.0 * spread), (8, 128))
        rate_ref[...] = rate
        one = rate[0:1, 0:1]
        hh, hl = split(h * (2.0 * one))
        hc_ref[...] = jnp.concatenate([hh, hl], 1)
        hs_ref[...] = jnp.broadcast_to(
            jnp.sum(h * h, 1, keepdims=True) * one, hs_ref.shape
        )
        mat_ref[...] = jnp.zeros_like(mat_ref)
        sum_ref[...] = jnp.zeros_like(sum_ref)
        kacc_ref[...] = jnp.zeros_like(kacc_ref)

    rate = rate_ref[0:1, 0:1]

    def weigh(x, at, kacc):
        u = jnp.exp2(x)
        u2 = u * u
        u4 = u2 * u2
        u8 = u4 * u4
        u16 = u8 * u8
        t4 = u16 + u16 + u8
        t3 = t4 + t4 + u4
        t2 = t3 + t3 + u2
        w = t2 + t2 + u
        k = (t4 + u16) + (t3 + t2)
        ws = w[:, 0:128]
        ks = k[:, 0:128]
        for q in range(1, w.shape[1] // 128):
            ws = ws + w[:, 128 * q : 128 * q + 128]
            ks = ks + k[:, 128 * q : 128 * q + 128]
        sum_ref[at, :] += ws
        for q in range(ks.shape[0] // 8):
            kacc = kacc + ks[8 * q : 8 * q + 8]
        return w, kacc

    def first(p):
        r = near_ref[p * cols : (p + 1) * cols, :]
        ip_ref[p % 2] = dot(hc_ref[...], jnp.concatenate([r, r], 1), NT)

    def second(p, kacc):
        sq = sq_ref[0:1, p * cols : (p + 1) * cols] * rate
        for c in range(flows // 16):
            at = slice(16 * c, 16 * c + 16)
            x = (ip_ref[p % 2, at, :] - sq) - jnp.tile(hs_ref[at, :], (1, cols // 128))
            w, kacc = weigh(x, at, kacc)
            wh_ref[p % 2, at, :] = w.astype(bf16)
        return kacc

    def third(p):
        mat_ref[...] += dot(wh_ref[p % 2], near_ref[p * cols : (p + 1) * cols, :], NN)

    count = near_ref.shape[0] // cols
    kacc = jnp.zeros((8, 128), f32)
    first(0)
    for p in range(count):
        if p + 1 < count:
            first(p + 1)
        kacc = second(p, kacc)
        if p > 0:
            third(p - 1)
    third(count - 1)
    kacc_ref[...] += kacc

    @pl.when(pl.program_id(0) == pl.num_programs(0) - 1)
    def _():
        h = h_ref[...]

        def finish(scale):
            total = jnp.sum(sum_ref[...], 1, keepdims=True)
            grad = (total * h - mat_ref[...]) * (rate * scale)
            lanes = jnp.sum(sum_ref[...], 0, keepdims=True) - jnp.sum(
                kacc_ref[...], 0, keepdims=True
            )
            return grad, jnp.sum(lanes, 1, keepdims=True)

        cross_g, cross_k = finish(4.0 / (total_real * LOG2E))
        mat_ref[...] = jnp.zeros_like(mat_ref)
        sum_ref[...] = jnp.zeros_like(sum_ref)
        kacc = jnp.zeros((8, 128), f32)
        rows_all = others_ref[...].reshape(-1, width)
        for p in range(rows_all.shape[0] // cols):
            rows = rows_all[p * cols : (p + 1) * cols]
            rh, rl = split(rows)
            hc = hc_ref[...]
            ip_ref[0] = dot(
                jnp.concatenate([hc, hc[:, :width]], 1),
                jnp.concatenate([rh, rh, rl], 1),
                NT,
            )
            sq = row_squares(rows)[0:1, :] * rate
            lows = []
            for c in range(flows // 16):
                at = slice(16 * c, 16 * c + 16)
                x = (ip_ref[0, at, :] - sq) - jnp.tile(hs_ref[at, :], (1, cols // 128))
                w, kacc = weigh(x, at, kacc)
                wh, wl = split(w)
                wh_ref[0, at, :] = wh
                wh_ref[1, at, :] = wl
            wh, wl = wh_ref[0], wh_ref[1]
            mat_ref[...] += dot(
                jnp.concatenate([wh, wl, wh], 1), jnp.concatenate([rh, rh, rl], 0), NN
            )
        kacc_ref[...] = kacc
        pair_g, pair_k = finish(-4.0 / (total_flows * LOG2E))
        grad = cross_g + pair_g
        loss = pair_k / (float(total_flows) * total_flows) - 2.0 * cross_k / (
            float(total_flows) * total_real
        )
        line = jnp.broadcast_to(loss, (EXTRA, width))
        for p in range(parts):
            out_ref[p, :share, :] = grad[p * share : (p + 1) * share]
            out_ref[p, share:, :] = line


def pair_sums(hall, others, near, sq, total_flows, total_real, block, cols):
    n, w = near.shape
    flows = hall.shape[0] * (hall.shape[1] - EXTRA)
    block = min(block, n)
    return pl.pallas_call(
        functools.partial(pair_kernel, cols, total_flows, total_real),
        grid=(n // block,),
        out_shape=jax.ShapeDtypeStruct(hall.shape, f32),
        in_specs=[
            fixed(hall.shape),
            fixed(others.shape),
            pl.BlockSpec((block, w), lambda i: (i, 0)),
            pl.BlockSpec((8, block), lambda i: (0, i)),
        ],
        out_specs=fixed(hall.shape),
        scratch_shapes=[
            VMEM((8, 128), f32),
            VMEM((flows, w), f32),
            VMEM((flows, 2 * w), bf16),
            VMEM((flows, 128), f32),
            VMEM((2, flows, cols), f32),
            VMEM((2, flows, cols), bf16),
            VMEM((flows, w), f32),
            VMEM((flows, 128), f32),
            VMEM((8, 128), f32),
        ],
        compiler_params=params(),
        cost_estimate=pl.CostEstimate(
            flops=6 * n * w * flows, bytes_accessed=2 * n * w, transcendentals=n * flows
        ),
    )(hall, others, near, sq)


def sum_kernel(parts_ref, out_ref):
    out_ref[...] = jnp.broadcast_to(jnp.sum(parts_ref[...], 0)[None], out_ref.shape)


def square_kernel(grad_ref, out_ref):
    grad = grad_ref[0 : grad_ref.shape[0] - EXTRA, :]
    lanes = jnp.sum(grad * grad, 0, keepdims=True)
    out_ref[...] = jnp.broadcast_to(jnp.sum(lanes, 1, keepdims=True), out_ref.shape)


def scale_kernel(grad_ref, sq_ref, out_ref, loss_ref):
    mean_sq = sq_ref[0:1, 0:1] * (1.0 / (HID_WIDTH * SEQ_STEPS))
    tall = out_ref.shape[0]
    out_ref[...] = grad_ref[0:tall, :] / jnp.sqrt(mean_sq + 1e-06)
    loss_ref[...] = grad_ref[tall:, 0:128]


def swap_sum(x, axis, count):
    hop = 1
    while hop < count:
        x = x + lax.ppermute(x, axis, [(i, i ^ hop) for i in range(count)])
        hop *= 2
    return x


def trade(x, axis):
    return lax.all_to_all(x, axis, 0, 0, tiled=True)


def per_device(real_count, gen_count, hidden, weight, lengths, real_rows):
    real_index = lax.axis_index("real")
    flows, width = hidden.shape
    local_steps = weight.shape[1]
    total_flows = flows * gen_count
    total_real = real_rows.shape[0] * real_count
    share = flows // real_count
    first = jnp.full((1,), real_index * local_steps, jnp.int32)
    counts, val, sig = call_once(
        count_kernel,
        [(flows, NUM_BINS), (local_steps, flows), (local_steps, flows)],
        first, weight.T, hidden, lengths[None, :], scalars=1,
    )
    parts = trade(counts.reshape(real_count, share, NUM_BINS), "real")
    own_len = lax.dynamic_slice_in_dim(lengths, real_index * share, share)[:, None]
    (own,) = call_once(share_kernel, [(gen_count, share, NUM_BINS)], parts, own_len)
    real_rows, own = lax.optimization_barrier((real_rows, own))
    others = trade(own, "gen")
    real_sums, near, sq = row_stats(real_rows, 2048)
    (load,) = call_once(
        load_kernel, [(real_count, share + EXTRA, NUM_BINS)], others, own, real_sums
    )
    hall = trade(load, "real")
    grad_part = pair_sums(hall, others, near, sq, total_flows, total_real, 4096, 256)
    (grad_own,) = call_once(sum_kernel, [grad_part.shape], trade(grad_part, "real"))
    part = back_steps(trade(grad_own, "real"), val, sig, hidden)
    grad = swap_sum(part, "gen", gen_count)
    (square,) = call_once(square_kernel, [(8, 128)], grad)
    square = swap_sum(square, "real", real_count)
    update, loss = call_once(
        scale_kernel, [(local_steps, width), (EXTRA, 128)], grad, square
    )
    return (update.T, loss[0, 0])


def solution(mesh):
    in_specs = (P("gen", None), P(None, "real"), P("gen"), P("real", None))
    out_specs = (P(None, "real"), P())
    body = functools.partial(per_device, mesh.shape["real"], mesh.shape["gen"])
    return jax.shard_map(
        body, mesh=mesh, in_specs=in_specs, out_specs=out_specs, check_vma=False
    )
```

```python
import functools
import math

import jax
import jax.numpy as jnp
from jax import lax
from jax.experimental import pallas as pl
from jax.experimental.pallas import tpu as pltpu
from jax.sharding import PartitionSpec as P

NUM_BINS = 256
SEQ_STEPS = 512
HID_WIDTH = 256
SPACING = 6.0 / NUM_BINS
LOG2E = math.log2(math.e)
UNIT = math.sqrt(LOG2E / 2.0) / SPACING
STEP = UNIT * SPACING
FAR = 1.0e6
EXTRA = 8

highest = lax.Precision.HIGHEST
f32 = jnp.float32
bf16 = jnp.bfloat16
NT = (((1,), (1,)), ((), ()))
NN = (((1,), (0,)), ((), ()))
VMEM = pltpu.VMEM
SMEM = pltpu.SMEM


def params(limit=48 << 20):
    return pltpu.CompilerParams(vmem_limit_bytes=limit)


def fixed(shape):
    return pl.BlockSpec(shape, lambda i: (0,) * len(shape))


def call_once(kernel, outs, *args, scalars=0, limit=48 << 20):
    return pl.pallas_call(
        kernel,
        grid=(1,),
        out_shape=[jax.ShapeDtypeStruct(s, f32) for s in outs],
        in_specs=[
            pl.BlockSpec(memory_space=SMEM) if i < scalars else fixed(a.shape)
            for i, a in enumerate(args)
        ],
        out_specs=[fixed(s) for s in outs],
        compiler_params=params(limit),
    )(*args)


def split(x):
    hi = x.astype(bf16)
    return hi, (x - hi.astype(f32)).astype(bf16)


def dot(a, b, dims):
    return lax.dot_general(a, b, dims, preferred_element_type=f32)


def count_kernel(first_ref, wt_ref, hid_ref, len_ref, out_ref, val_ref, sig_ref):
    pre = lax.dot_general(
        wt_ref[...], hid_ref[...], NT, precision=highest, preferred_element_type=f32
    )
    small = jnp.exp(-jnp.abs(pre))
    steps = jnp.maximum(pre, 0.0) + jnp.log1p(small)
    at = first_ref[0] + lax.broadcasted_iota(jnp.int32, pre.shape, 0)
    lens = len_ref[...]
    val = jnp.where(at < lens, steps * UNIT, FAR)
    val_ref[...] = val
    sig = 1.0 / (1.0 + jnp.exp(-pre))
    sig_ref[...] = sig / (lens.astype(f32) * (UNIT * SPACING * SPACING))

    def bins(i, carry):
        base = (8 * i).astype(f32) + 0.5
        rows = []
        for j in range(8):
            off = (base + j) * STEP - val
            e = jnp.exp2(-(off * off))
            rows.append(jnp.sum(e, 0, keepdims=True))
        out_ref[pl.ds(pl.multiple_of(8 * i, 8), 8), :] = jnp.concatenate(rows, 0)
        return carry

    lax.fori_loop(0, NUM_BINS // 8, bins, 0)
    out_ref[...] = out_ref[...].T


def back_kernel(gh_ref, val_ref, sig_ref, hid_ref, out_ref, ght_ref):
    parts, share = gh_ref.shape[0], gh_ref.shape[1] - EXTRA
    tall = val_ref.shape[0]
    gh = jnp.concatenate([gh_ref[p, :share, :] for p in range(parts)], 0)
    ght_ref[...] = gh.T
    val = val_ref[...]

    def bins(i, acc):
        base = (8 * i).astype(f32) + 0.5
        rows = ght_ref[pl.ds(pl.multiple_of(8 * i, 8), 8), :]
        for j in range(8):
            off = (base + j) * STEP - val
            e = jnp.exp2(-(off * off))
            acc = acc + (e * off) * rows[j : j + 1, :]
        return acc

    slope = lax.fori_loop(0, NUM_BINS // 8, bins, jnp.zeros_like(val))
    out_ref[0:tall, :] = lax.dot_general(
        slope * sig_ref[...], hid_ref[...], NN, precision=highest, preferred_element_type=f32
    )
    out_ref[tall:, :] = gh_ref[0, share:, :]


def back_steps(gh, val, sig, hidden):
    t, g = val.shape
    z = hidden.shape[1]
    return pl.pallas_call(
        back_kernel,
        grid=(1,),
        out_shape=jax.ShapeDtypeStruct((t + EXTRA, z), f32),
        in_specs=[fixed(gh.shape), fixed((t, g)), fixed((t, g)), fixed((g, z))],
        out_specs=fixed((t + EXTRA, z)),
        scratch_shapes=[VMEM((NUM_BINS, g), f32)],
        compiler_params=params(),
    )(gh, val, sig, hidden)


def row_squares(squares):
    hi, lo = split(squares)
    ones = jnp.ones((8, 2 * squares.shape[1]), bf16)
    return dot(ones, jnp.concatenate([hi, lo], 1), NT)


def stat_kernel(rows_ref, sum_ref, sq_ref):
    rows = rows_ref[...]
    w = rows.shape[1]
    near = rows.astype(bf16).astype(f32)
    near = near * near
    half = w // 2
    sq_ref[...] = row_squares(near[:, :half] + near[:, half:])
    part = jnp.concatenate(
        [
            jnp.sum(rows.reshape(-1, 8, w), 0),
            jnp.sum((rows * rows).reshape(-1, 8, w), 0),
        ],
        0,
    )

    @pl.when(pl.program_id(0) == 0)
    def _():
        sum_ref[...] = part

    @pl.when(pl.program_id(0) > 0)
    def _():
        sum_ref[...] += part


def row_stats(rows, block, start, count):
    w = rows.shape[1]
    return pl.pallas_call(
        stat_kernel,
        grid=(count,),
        out_shape=[
            jax.ShapeDtypeStruct((16, w), f32),
            jax.ShapeDtypeStruct((8, count * block), f32),
        ],
        in_specs=[pl.BlockSpec((block, w), lambda i: (start + i, 0))],
        out_specs=[
            fixed((16, w)),
            pl.BlockSpec((8, block), lambda i: (0, i)),
        ],
        compiler_params=params(),
        cost_estimate=pl.CostEstimate(
            flops=16 * count * block * w, bytes_accessed=4 * count * block * w, transcendentals=0
        ),
    )(rows)


def share_kernel(parts_ref, len_ref, out_ref):
    count = jnp.sum(parts_ref[...], 0)
    hist = count / len_ref[...].astype(f32)
    out_ref[...] = jnp.broadcast_to(hist[None], out_ref.shape)


def load_kernel(others_ref, more_ref, own_ref, front_ref, back_ref, out_ref):
    parts, share, w = others_ref.shape
    rows = jnp.concatenate(
        [r[...].reshape(parts * share, w) for r in (others_ref, more_ref)], 0
    )
    stats = jnp.concatenate(
        [
            jnp.sum(rows, 0, keepdims=True),
            jnp.sum(rows * rows, 0, keepdims=True),
            jnp.sum(front_ref[0:8, :] + back_ref[0:8, :], 0, keepdims=True),
            jnp.sum(front_ref[8:16, :] + back_ref[8:16, :], 0, keepdims=True),
            jnp.zeros((EXTRA - 4, w), f32),
        ],
        0,
    )
    load = jnp.concatenate([own_ref[0], stats], 0)
    out_ref[...] = jnp.broadcast_to(load[None], out_ref.shape)


def pair_kernel(
    cols, total_flows, total_real, hall_ref, others_ref, more_ref, rows_ref, front_ref, back_ref, out_ref,
    rate_ref, h_ref, hc_ref, hs_ref, ip_ref, wh_ref, mat_ref, sum_ref, kacc_ref, near_ref, sq_ref,
):
    parts, tall, width = hall_ref.shape
    share = tall - EXTRA
    flows = parts * share

    @pl.when(pl.program_id(0) == 0)
    def _():
        h = jnp.concatenate([hall_ref[p, :share, :] for p in range(parts)], 0)
        h_ref[...] = h
        stats = hall_ref[0, share:, :]
        for p in range(1, parts):
            stats = stats + hall_ref[p, share:, :]
        line = (
            stats[1:2, :] / total_flows
            + stats[3:4, :] / total_real
            - 2.0 * ((stats[0:1, :] / total_flows) * (stats[2:3, :] / total_real))
        )
        spread = jnp.sum(line, 1, keepdims=True)
        rate = jnp.broadcast_to(LOG2E / (4.0 * spread), (8, 128))
        rate_ref[...] = rate
        one = rate[0:1, 0:1]
        hh, hl = split(h * (2.0 * one))
        hc_ref[...] = jnp.concatenate([hh, hl], 1)
        hs_ref[...] = jnp.broadcast_to(
            jnp.sum(h * h, 1, keepdims=True) * one, hs_ref.shape
        )
        mat_ref[...] = jnp.zeros_like(mat_ref)
        sum_ref[...] = jnp.zeros_like(sum_ref)
        kacc_ref[...] = jnp.zeros_like(kacc_ref)

    rate = rate_ref[0:1, 0:1]

    def weigh(x, at, kacc):
        u = jnp.exp2(x)
        u2 = u * u
        u4 = u2 * u2
        u8 = u4 * u4
        u16 = u8 * u8
        t4 = u16 + u16 + u8
        t3 = t4 + t4 + u4
        t2 = t3 + t3 + u2
        w = t2 + t2 + u
        k = (t4 + u16) + (t3 + t2)
        ws = w[:, 0:128]
        ks = k[:, 0:128]
        for q in range(1, w.shape[1] // 128):
            ws = ws + w[:, 128 * q : 128 * q + 128]
            ks = ks + k[:, 128 * q : 128 * q + 128]
        sum_ref[at, :] += ws
        for q in range(ks.shape[0] // 8):
            kacc = kacc + ks[8 * q : 8 * q + 8]
        return w, kacc

    early = pl.program_id(0) < pl.num_programs(0) // 2
    sq_ref[...] = jnp.where(early, front_ref[0:1, :], back_ref[0:1, :]) * rate

    def first(p):
        r = rows_ref[p * cols : (p + 1) * cols, :].astype(bf16)
        near_ref[p % 3] = r
        ip_ref[p % 2] = dot(hc_ref[...], jnp.concatenate([r, r], 1), NT)

    def second(p, kacc):
        sq = sq_ref[0:1, p * cols : (p + 1) * cols]
        for c in range(flows // 16):
            at = slice(16 * c, 16 * c + 16)
            x = (ip_ref[p % 2, at, :] - sq) - jnp.tile(hs_ref[at, :], (1, cols // 128))
            w, kacc = weigh(x, at, kacc)
            wh_ref[p % 2, at, :] = w.astype(bf16)
        return kacc

    def third(p):
        mat_ref[...] += dot(wh_ref[p % 2], near_ref[p % 3], NN)

    count = rows_ref.shape[0] // cols
    kacc = jnp.zeros((8, 128), f32)
    first(0)
    for p in range(count):
        if p + 1 < count:
            first(p + 1)
        kacc = second(p, kacc)
        if p > 0:
            third(p - 1)
    third(count - 1)
    kacc_ref[...] += kacc

    @pl.when(pl.program_id(0) == pl.num_programs(0) - 1)
    def _():
        h = h_ref[...]

        def finish(scale):
            total = jnp.sum(sum_ref[...], 1, keepdims=True)
            grad = (total * h - mat_ref[...]) * (rate * scale)
            lanes = jnp.sum(sum_ref[...], 0, keepdims=True) - jnp.sum(
                kacc_ref[...], 0, keepdims=True
            )
            return grad, jnp.sum(lanes, 1, keepdims=True)

        cross_g, cross_k = finish(4.0 / (total_real * LOG2E))
        mat_ref[...] = jnp.zeros_like(mat_ref)
        sum_ref[...] = jnp.zeros_like(sum_ref)
        kacc = jnp.zeros((8, 128), f32)
        rows_all = jnp.concatenate(
            [r[...].reshape(-1, width) for r in (others_ref, more_ref)], 0
        )
        for p in range(rows_all.shape[0] // cols):
            rows = rows_all[p * cols : (p + 1) * cols]
            rh, rl = split(rows)
            hc = hc_ref[...]
            ip_ref[0] = dot(
                jnp.concatenate([hc, hc[:, :width]], 1),
                jnp.concatenate([rh, rh, rl], 1),
                NT,
            )
            sq = row_squares(rows * rows)[0:1, :] * rate
            lows = []
            for c in range(flows // 16):
                at = slice(16 * c, 16 * c + 16)
                x = (ip_ref[0, at, :] - sq) - jnp.tile(hs_ref[at, :], (1, cols // 128))
                w, kacc = weigh(x, at, kacc)
                wh, wl = split(w)
                wh_ref[0, at, :] = wh
                wh_ref[1, at, :] = wl
            wh, wl = wh_ref[0], wh_ref[1]
            mat_ref[...] += dot(
                jnp.concatenate([wh, wl, wh], 1), jnp.concatenate([rh, rh, rl], 0), NN
            )
        kacc_ref[...] = kacc
        pair_g, pair_k = finish(-4.0 / (total_flows * LOG2E))
        grad = cross_g + pair_g
        loss = pair_k / (float(total_flows) * total_flows) - 2.0 * cross_k / (
            float(total_flows) * total_real
        )
        line = jnp.broadcast_to(loss, (EXTRA, width))
        for p in range(parts):
            out_ref[p, :share, :] = grad[p * share : (p + 1) * share]
            out_ref[p, share:, :] = line


def pair_sums(hall, others, more, rows, front, back, total_flows, total_real, block, cols):
    n, w = rows.shape
    flows = hall.shape[0] * (hall.shape[1] - EXTRA)
    half = n // block // 2
    return pl.pallas_call(
        functools.partial(pair_kernel, cols, total_flows, total_real),
        grid=(2 * half,),
        out_shape=jax.ShapeDtypeStruct(hall.shape, f32),
        in_specs=[
            fixed(hall.shape),
            fixed(others.shape),
            fixed(more.shape),
            pl.BlockSpec((block, w), lambda i: (i, 0)),
            pl.BlockSpec((8, block), lambda i: (0, jnp.minimum(i, half - 1))),
            pl.BlockSpec((8, block), lambda i: (0, jnp.maximum(i - half, 0))),
        ],
        out_specs=fixed(hall.shape),
        scratch_shapes=[
            VMEM((8, 128), f32),
            VMEM((flows, w), f32),
            VMEM((flows, 2 * w), bf16),
            VMEM((flows, 128), f32),
            VMEM((2, flows, cols), f32),
            VMEM((2, flows, cols), bf16),
            VMEM((flows, w), f32),
            VMEM((flows, 128), f32),
            VMEM((8, 128), f32),
            VMEM((3, cols, w), bf16),
            VMEM((1, block), f32),
        ],
        compiler_params=params(),
        cost_estimate=pl.CostEstimate(
            flops=6 * n * w * flows, bytes_accessed=4 * n * w, transcendentals=n * flows
        ),
    )(hall, others, more, rows, front, back)


def sum_kernel(parts_ref, out_ref):
    out_ref[...] = jnp.broadcast_to(jnp.sum(parts_ref[...], 0)[None], out_ref.shape)


def square_kernel(grad_ref, out_ref):
    grad = grad_ref[0 : grad_ref.shape[0] - EXTRA, :]
    lanes = jnp.sum(grad * grad, 0, keepdims=True)
    out_ref[...] = jnp.broadcast_to(jnp.sum(lanes, 1, keepdims=True)[None], out_ref.shape)


def scale_kernel(grad_ref, sq_ref, out_ref, loss_ref):
    mean_sq = jnp.sum(sq_ref[...], 0)[0:1, 0:1] * (1.0 / (HID_WIDTH * SEQ_STEPS))
    tall = out_ref.shape[0]
    out_ref[...] = grad_ref[0:tall, :] / jnp.sqrt(mean_sq + 1e-06)
    loss_ref[0] = jnp.max(grad_ref[tall : tall + 1, 0:128])


def swap_sum(x, axis, count, groups):
    for hops in groups:
        sent = [lax.ppermute(x, axis, [(i, i ^ hop) for i in range(count)]) for hop in hops]
        for other in sent:
            x = x + other
    return x


def trade(x, axis, groups=None):
    return lax.all_to_all(x, axis, 0, 0, axis_index_groups=groups, tiled=True)


def per_device(real_count, gen_count, hidden, weight, lengths, real_rows):
    real_index = lax.axis_index("real")
    flows, width = hidden.shape
    local_steps = weight.shape[1]
    total_flows = flows * gen_count
    total_real = real_rows.shape[0] * real_count
    share = flows // real_count
    block = min(4096, real_rows.shape[0] // 2)
    half = real_rows.shape[0] // block // 2
    first = jnp.full((1,), real_index * local_steps, jnp.int32)
    counts, val, sig = call_once(
        count_kernel,
        [(flows, NUM_BINS), (local_steps, flows), (local_steps, flows)],
        first, weight.T, hidden, lengths[None, :], scalars=1, limit=60 << 20,
    )
    rows_early, counts = lax.optimization_barrier((real_rows, counts))
    parts = trade(counts.reshape(real_count, share, NUM_BINS), "real")
    front_sums, front_sq = row_stats(rows_early, block, 0, half)
    own_len = lax.dynamic_slice_in_dim(lengths, real_index * share, share)[:, None]
    own_len, front_sums = lax.optimization_barrier((own_len, front_sums))
    (own,) = call_once(share_kernel, [(gen_count // 2, share, NUM_BINS)], parts, own_len)
    same = [list(range(c, gen_count, 2)) for c in range(2)]
    rows_late, own = lax.optimization_barrier((real_rows, own))
    near_rows = trade(own, "gen", same)
    back_sums, back_sq = row_stats(rows_late, block, half, half)
    near_rows, back_sums = lax.optimization_barrier((near_rows, back_sums))
    far_rows = lax.ppermute(near_rows, "gen", [(i, i ^ 1) for i in range(gen_count)])
    (load,) = call_once(
        load_kernel,
        [(real_count, share + EXTRA, NUM_BINS)],
        near_rows, far_rows, own, front_sums, back_sums,
    )
    hall = trade(load, "real")
    grad_part = pair_sums(
        hall, near_rows, far_rows, real_rows, front_sq, back_sq, total_flows, total_real, block, 256
    )
    (grad_own,) = call_once(sum_kernel, [grad_part.shape], trade(grad_part, "real"))
    part = back_steps(trade(grad_own, "real"), val, sig, hidden)
    grad = swap_sum(part, "gen", gen_count, ((1,), (2,), (4, 8, 12)))
    (square,) = call_once(square_kernel, [(real_count, 8, 128)], grad)
    update, loss = pl.pallas_call(
        scale_kernel,
        grid=(1,),
        out_shape=[
            jax.ShapeDtypeStruct((local_steps, width), f32),
            jax.ShapeDtypeStruct((1,), f32),
        ],
        in_specs=[fixed(grad.shape), fixed(square.shape)],
        out_specs=[fixed((local_steps, width)), pl.BlockSpec(memory_space=SMEM)],
        compiler_params=params(),
    )(grad, trade(square, "real"))
    return (update.T, loss.reshape(()))


def solution(mesh):
    in_specs = (P("gen", None), P(None, "real"), P("gen"), P("real", None))
    out_specs = (P(None, "real"), P())
    body = functools.partial(per_device, mesh.shape["real"], mesh.shape["gen"])
    return jax.shard_map(
        body, mesh=mesh, in_specs=in_specs, out_specs=out_specs, check_vma=False
    )
```

```python
import functools
import math

import jax
import jax.numpy as jnp
from jax import lax
from jax.experimental import pallas as pl
from jax.experimental.pallas import tpu as pltpu
from jax.sharding import PartitionSpec as P

NUM_BINS = 256
SEQ_STEPS = 512
HID_WIDTH = 256
SPACING = 6.0 / NUM_BINS
LOG2E = math.log2(math.e)
UNIT = math.sqrt(LOG2E / 2.0) / SPACING
STEP = UNIT * SPACING
FAR = 1.0e6
EXTRA = 8
ROOT_2 = math.sqrt(1.0 / 2.0)
ROOT_8 = math.sqrt(1.0 / 8.0)

highest = lax.Precision.HIGHEST
f32 = jnp.float32
bf16 = jnp.bfloat16
NT = (((1,), (1,)), ((), ()))
NN = (((1,), (0,)), ((), ()))
VMEM = pltpu.VMEM
SMEM = pltpu.SMEM


def params(limit=48 << 20):
    return pltpu.CompilerParams(vmem_limit_bytes=limit)


def whole():
    return pl.BlockSpec(memory_space=VMEM)


def fixed(shape):
    return pl.BlockSpec(shape, lambda i: (0,) * len(shape))


def call_once(kernel, outs, *args, scalars=0, limit=48 << 20):
    return pl.pallas_call(
        kernel,
        grid=(1,),
        out_shape=[jax.ShapeDtypeStruct(s, f32) for s in outs],
        in_specs=[
            pl.BlockSpec(memory_space=SMEM) if i < scalars else fixed(a.shape)
            for i, a in enumerate(args)
        ],
        out_specs=[fixed(s) for s in outs],
        compiler_params=params(limit),
    )(*args)


def split(x):
    hi = x.astype(bf16)
    return hi, (x - hi.astype(f32)).astype(bf16)


def dot(a, b, dims):
    return lax.dot_general(a, b, dims, preferred_element_type=f32)


def count_kernel(first_ref, wt_ref, hid_ref, len_ref, out_ref, val_ref, sig_ref):
    pre = lax.dot_general(
        wt_ref[...], hid_ref[...], NT, precision=highest, preferred_element_type=f32
    )
    small = jnp.exp(-jnp.abs(pre))
    steps = jnp.maximum(pre, 0.0) + jnp.log1p(small)
    at = first_ref[0] + lax.broadcasted_iota(jnp.int32, pre.shape, 0)
    lens = len_ref[...]
    val = jnp.where(at < lens, steps * UNIT, FAR)
    val_ref[...] = val
    sig = 1.0 / (1.0 + jnp.exp(-pre))
    sig_ref[...] = sig / (lens.astype(f32) * (UNIT * SPACING * SPACING))

    def bins(i, carry):
        base = (8 * i).astype(f32) + 0.5
        rows = []
        for j in range(8):
            off = (base + j) * STEP - val
            e = jnp.exp2(-(off * off))
            rows.append(jnp.sum(e, 0, keepdims=True))
        out_ref[pl.ds(pl.multiple_of(8 * i, 8), 8), :] = jnp.concatenate(rows, 0)
        return carry

    lax.fori_loop(0, NUM_BINS // 8, bins, 0)
    out_ref[...] = out_ref[...].T


def back_kernel(gh_ref, val_ref, sig_ref, hid_ref, out_ref, ght_ref):
    parts, share = gh_ref.shape[0], gh_ref.shape[1] - EXTRA
    tall = val_ref.shape[0]
    gh = jnp.concatenate([gh_ref[p, :share, :] for p in range(parts)], 0)
    ght_ref[...] = gh.T
    val = val_ref[...]

    def bins(i, acc):
        base = (8 * i).astype(f32) + 0.5
        rows = ght_ref[pl.ds(pl.multiple_of(8 * i, 8), 8), :]
        for j in range(8):
            off = (base + j) * STEP - val
            e = jnp.exp2(-(off * off))
            acc = acc + (e * off) * rows[j : j + 1, :]
        return acc

    slope = lax.fori_loop(0, NUM_BINS // 8, bins, jnp.zeros_like(val))
    out_ref[0:tall, :] = lax.dot_general(
        slope * sig_ref[...], hid_ref[...], NN, precision=highest, preferred_element_type=f32
    )
    out_ref[tall:, :] = gh_ref[0, share:, :]


def back_steps(gh, val, sig, hidden):
    t, g = val.shape
    z = hidden.shape[1]
    return pl.pallas_call(
        back_kernel,
        grid=(1,),
        out_shape=jax.ShapeDtypeStruct((t + EXTRA, z), f32),
        in_specs=[fixed(gh.shape), fixed((t, g)), fixed((t, g)), fixed((g, z))],
        out_specs=fixed((t + EXTRA, z)),
        scratch_shapes=[VMEM((NUM_BINS, g), f32)],
        compiler_params=params(),
    )(gh, val, sig, hidden)


def row_squares(squares):
    hi, lo = split(squares)
    ones = jnp.ones((8, 2 * squares.shape[1]), bf16)
    return dot(ones, jnp.concatenate([hi, lo], 1), NT)


def stat_kernel(rows_ref, sum_ref, sq_ref):
    rows = rows_ref[...]
    w = rows.shape[1]
    near = rows.astype(bf16).astype(f32)
    near = near * near
    half = w // 2
    sq_ref[...] = row_squares(near[:, :half] + near[:, half:])
    part = jnp.concatenate(
        [
            jnp.sum(rows.reshape(-1, 8, w), 0),
            jnp.sum((rows * rows).reshape(-1, 8, w), 0),
        ],
        0,
    )

    @pl.when(pl.program_id(0) == 0)
    def _():
        sum_ref[...] = part

    @pl.when(pl.program_id(0) > 0)
    def _():
        sum_ref[...] += part


def row_stats(rows, block, start, count):
    w = rows.shape[1]
    return pl.pallas_call(
        stat_kernel,
        grid=(count,),
        out_shape=[
            jax.ShapeDtypeStruct((16, w), f32),
            jax.ShapeDtypeStruct((8, count * block), f32),
        ],
        in_specs=[pl.BlockSpec((block, w), lambda i: (start + i, 0))],
        out_specs=[
            fixed((16, w)),
            pl.BlockSpec((8, block), lambda i: (0, i)),
        ],
        compiler_params=params(),
        cost_estimate=pl.CostEstimate(
            flops=16 * count * block * w, bytes_accessed=4 * count * block * w, transcendentals=0
        ),
    )(rows)


def near_kernel(rows_ref, out_ref):
    out_ref[...] = rows_ref[...].astype(bf16)


def near_rows_of(rows, block, count):
    w = rows.shape[1]
    return pl.pallas_call(
        near_kernel,
        grid=(count,),
        out_shape=jax.ShapeDtypeStruct((count * block, w), bf16),
        in_specs=[pl.BlockSpec((block, w), lambda i: (i, 0))],
        out_specs=pl.BlockSpec((block, w), lambda i: (i, 0)),
        compiler_params=params(),
        cost_estimate=pl.CostEstimate(
            flops=count * block * w, bytes_accessed=4 * count * block * w, transcendentals=0
        ),
    )(rows)


def share_kernel(parts_ref, len_ref, out_ref):
    count = jnp.sum(parts_ref[...], 0)
    hist = count / len_ref[...].astype(f32)
    out_ref[...] = jnp.broadcast_to(hist[None], out_ref.shape)


def load_kernel(others_ref, more_ref, own_ref, front_ref, back_ref, out_ref):
    parts, share, w = others_ref.shape
    rows = jnp.concatenate(
        [r[...].reshape(parts * share, w) for r in (others_ref, more_ref)], 0
    )
    stats = jnp.concatenate(
        [
            jnp.sum(rows, 0, keepdims=True),
            jnp.sum(rows * rows, 0, keepdims=True),
            jnp.sum(front_ref[0:8, :] + back_ref[0:8, :], 0, keepdims=True),
            jnp.sum(front_ref[8:16, :] + back_ref[8:16, :], 0, keepdims=True),
            jnp.zeros((EXTRA - 4, w), f32),
        ],
        0,
    )
    load = jnp.concatenate([own_ref[0], stats], 0)
    out_ref[...] = jnp.broadcast_to(load[None], out_ref.shape)


def pair_kernel(
    cols, total_flows, total_real, hall_ref, others_ref, more_ref, front_ref, rows_ref,
    front_sq_ref, back_sq_ref, out_ref,
    rate_ref, h_ref, hc_ref, hs_ref, ip_ref, wh_ref, mat_ref, sum_ref, kacc_ref, held_ref, near_ref, sems,
):
    parts, tall, width = hall_ref.shape
    share = tall - EXTRA
    flows = parts * share
    front = front_ref.shape[0]
    rest = [
        pltpu.make_async_copy(
            rows_ref.at[pl.ds(at, at), :], held_ref.at[pl.ds(at - front, at), :], sems.at[c]
        )
        for c, at in enumerate((front, 2 * front, 4 * front))
    ]
    rest[0].start()
    rest[1].start()

    def prepare():
        h = jnp.concatenate([hall_ref[p, :share, :] for p in range(parts)], 0)
        h_ref[...] = h
        stats = hall_ref[0, share:, :]
        for p in range(1, parts):
            stats = stats + hall_ref[p, share:, :]
        line = (
            stats[1:2, :] / total_flows
            + stats[3:4, :] / total_real
            - 2.0 * ((stats[0:1, :] / total_flows) * (stats[2:3, :] / total_real))
        )
        spread = jnp.sum(line, 1, keepdims=True)
        rate = jnp.broadcast_to(LOG2E / (4.0 * spread), (8, 128))
        rate_ref[...] = rate
        one = rate[0:1, 0:1]
        hh, hl = split(h * (2.0 * one))
        hc_ref[...] = jnp.concatenate([hh, hl], 1)
        hs_ref[...] = jnp.broadcast_to(
            jnp.sum(h * h, 1, keepdims=True) * one - 1.0, hs_ref.shape
        )
        mat_ref[...] = jnp.zeros_like(mat_ref)
        sum_ref[...] = jnp.zeros_like(sum_ref)
        kacc_ref[...] = jnp.zeros_like(kacc_ref)

    prepare()
    rate = rate_ref[0:1, 0:1]

    def weigh(x, at, sums):
        a = jnp.exp2(x)
        a2 = a * a
        b = a2 * ROOT_2
        b = b * b
        c = b * 0.5
        c = c * c
        d = c * ROOT_8
        d = d * d
        w = (a + a2) + (b + c) + d

        def fold(v):
            t = v[:, 0:128]
            for q in range(1, v.shape[1] // 128):
                t = t + v[:, 128 * q : 128 * q + 128]
            return t

        sum_ref[at, :] += fold(w)
        out = []
        for v, total in zip((a2, b, c, d), sums):
            t = fold(v)
            for q in range(t.shape[0] // 8):
                total = total + t[8 * q : 8 * q + 8]
            out.append(total)
        return w, tuple(out)

    early = front // cols

    def first(p):
        if p < early:
            r = front_ref[p * cols : (p + 1) * cols, :]
        else:
            r = held_ref[(p - early) * cols : (p - early + 1) * cols, :].astype(bf16)
            near_ref[p % 3] = r
        ip_ref[p % 2] = dot(hc_ref[...], jnp.concatenate([r, r], 1), NT)

    def second(p, sums):
        ref, q = (front_sq_ref, p) if p < 4 * early else (back_sq_ref, p - 4 * early)
        sq = ref[0:1, q * cols : (q + 1) * cols] * rate
        for c in range(flows // 16):
            at = slice(16 * c, 16 * c + 16)
            x = (ip_ref[p % 2, at, :] - sq) - jnp.tile(hs_ref[at, :], (1, cols // 128))
            w, sums = weigh(x, at, sums)
            wh_ref[p % 2, at, :] = w.astype(bf16)
        return sums

    def third(p):
        if p < early:
            r = front_ref[p * cols : (p + 1) * cols, :]
        else:
            r = near_ref[p % 3]
        mat_ref[...] += dot(wh_ref[p % 2], r, NN)

    def keep(sums):
        for q in range(4):
            kacc_ref[8 * q : 8 * q + 8, :] += sums[q]

    zeros = (jnp.zeros((8, 128), f32),) * 4
    count = early + held_ref.shape[0] // cols
    sums = zeros
    first(0)
    for p in range(count):
        if p + 1 == early:
            rest[0].wait()
            rest[2].start()
        if p + 1 == 2 * early:
            rest[1].wait()
        if p + 1 == 4 * early:
            rest[2].wait()
        if p + 1 < count:
            first(p + 1)
        sums = second(p, sums)
        if p % 16 == 15:
            keep(sums)
            sums = zeros
        if p > 0:
            third(p - 1)
    third(count - 1)
    keep(sums)

    def complete():
        h = h_ref[...]

        def finish(scale):
            total = jnp.sum(sum_ref[...], 1, keepdims=True)
            grad = (total * h - mat_ref[...]) * (rate * (0.5 * scale))
            lanes = 0.5 * jnp.sum(sum_ref[...], 0, keepdims=True)
            for q, part in enumerate((1 / 4, 3 / 8, 7 / 16, 15 / 32)):
                lanes = lanes - part * jnp.sum(kacc_ref[8 * q : 8 * q + 8, :], 0, keepdims=True)
            return grad, jnp.sum(lanes, 1, keepdims=True)

        cross_g, cross_k = finish(4.0 / (total_real * LOG2E))
        mat_ref[...] = jnp.zeros_like(mat_ref)
        sum_ref[...] = jnp.zeros_like(sum_ref)
        kacc_ref[...] = jnp.zeros_like(kacc_ref)
        sums = zeros
        rows_all = jnp.concatenate(
            [r[...].reshape(-1, width) for r in (others_ref, more_ref)], 0
        )
        for p in range(rows_all.shape[0] // cols):
            rows = rows_all[p * cols : (p + 1) * cols]
            rh, rl = split(rows)
            hc = hc_ref[...]
            ip_ref[0] = dot(
                jnp.concatenate([hc, hc[:, :width]], 1),
                jnp.concatenate([rh, rh, rl], 1),
                NT,
            )
            sq = row_squares(rows * rows)[0:1, :] * rate
            for c in range(flows // 16):
                at = slice(16 * c, 16 * c + 16)
                x = (ip_ref[0, at, :] - sq) - jnp.tile(hs_ref[at, :], (1, cols // 128))
                w, sums = weigh(x, at, sums)
                wh, wl = split(w)
                wh_ref[0, at, :] = wh
                wh_ref[1, at, :] = wl
            wh, wl = wh_ref[0], wh_ref[1]
            mat_ref[...] += dot(
                jnp.concatenate([wh, wl, wh], 1), jnp.concatenate([rh, rh, rl], 0), NN
            )
        keep(sums)
        pair_g, pair_k = finish(-4.0 / (total_flows * LOG2E))
        grad = cross_g + pair_g
        loss = pair_k / (float(total_flows) * total_flows) - 2.0 * cross_k / (
            float(total_flows) * total_real
        )
        line = jnp.broadcast_to(loss, (EXTRA, width))
        for p in range(parts):
            out_ref[p, :share, :] = grad[p * share : (p + 1) * share]
            out_ref[p, share:, :] = line

    complete()


def pair_sums(hall, others, more, front, rows, front_sq, back_sq, total_flows, total_real, cols):
    n, w = rows.shape
    flows = hall.shape[0] * (hall.shape[1] - EXTRA)
    return pl.pallas_call(
        functools.partial(pair_kernel, cols, total_flows, total_real),
        grid=(1,),
        out_shape=jax.ShapeDtypeStruct(hall.shape, f32),
        in_specs=[
            fixed(hall.shape),
            fixed(others.shape),
            fixed(more.shape),
            whole(),
            pl.BlockSpec(memory_space=pl.ANY),
            fixed(front_sq.shape),
            fixed(back_sq.shape),
        ],
        out_specs=fixed(hall.shape),
        scratch_shapes=[
            VMEM((8, 128), f32),
            VMEM((flows, w), f32),
            VMEM((flows, 2 * w), bf16),
            VMEM((flows, 128), f32),
            VMEM((2, flows, cols), f32),
            VMEM((2, flows, cols), bf16),
            VMEM((flows, w), f32),
            VMEM((flows, 128), f32),
            VMEM((32, 128), f32),
            VMEM((n - front.shape[0], w), f32),
            VMEM((3, cols, w), bf16),
            pltpu.SemaphoreType.DMA((3,)),
        ],
        compiler_params=params(),
        cost_estimate=pl.CostEstimate(
            flops=6 * n * w * flows, bytes_accessed=4 * n * w, transcendentals=n * flows
        ),
    )(hall, others, more, front, rows, front_sq, back_sq)


def sum_kernel(parts_ref, out_ref):
    out_ref[...] = jnp.broadcast_to(jnp.sum(parts_ref[...], 0)[None], out_ref.shape)


def square_kernel(grad_ref, out_ref):
    grad = grad_ref[0 : grad_ref.shape[0] - EXTRA, :]
    lanes = jnp.sum(grad * grad, 0, keepdims=True)
    out_ref[...] = jnp.broadcast_to(jnp.sum(lanes, 1, keepdims=True)[None], out_ref.shape)


def scale_kernel(grad_ref, sq_ref, out_ref, loss_ref):
    mean_sq = jnp.sum(sq_ref[...], 0)[0:1, 0:1] * (1.0 / (HID_WIDTH * SEQ_STEPS))
    tall = out_ref.shape[0]
    out_ref[...] = grad_ref[0:tall, :] / jnp.sqrt(mean_sq + 1e-06)
    loss_ref[0] = jnp.max(grad_ref[tall : tall + 1, 0:128])


def swap_sum(x, axis, count, groups):
    for hops in groups:
        sent = [lax.ppermute(x, axis, [(i, i ^ hop) for i in range(count)]) for hop in hops]
        for other in sent:
            x = x + other
    return x


def trade(x, axis, groups=None):
    return lax.all_to_all(x, axis, 0, 0, axis_index_groups=groups, tiled=True)


def per_device(real_count, gen_count, hidden, weight, lengths, real_rows):
    real_index = lax.axis_index("real")
    flows, width = hidden.shape
    local_steps = weight.shape[1]
    total_flows = flows * gen_count
    total_real = real_rows.shape[0] * real_count
    share = flows // real_count
    block = min(4096, real_rows.shape[0] // 2)
    half = real_rows.shape[0] // block // 2
    first = jnp.full((1,), real_index * local_steps, jnp.int32)
    counts, val, sig = call_once(
        count_kernel,
        [(flows, NUM_BINS), (local_steps, flows), (local_steps, flows)],
        first, weight.T, hidden, lengths[None, :], scalars=1, limit=60 << 20,
    )
    rows_early, counts = lax.optimization_barrier((real_rows, counts))
    parts = trade(counts.reshape(real_count, share, NUM_BINS), "real")
    front_sums, front_sq = row_stats(rows_early, block, 0, half)
    own_len = lax.dynamic_slice_in_dim(lengths, real_index * share, share)[:, None]
    own_len, front_sums = lax.optimization_barrier((own_len, front_sums))
    (own,) = call_once(share_kernel, [(gen_count // 2, share, NUM_BINS)], parts, own_len)
    same = [list(range(c, gen_count, 2)) for c in range(2)]
    rows_late, own = lax.optimization_barrier((real_rows, own))
    near_rows = trade(own, "gen", same)
    back_sums, back_sq = row_stats(rows_late, block, half, half)
    near_rows, back_sums = lax.optimization_barrier((near_rows, back_sums))
    far_rows = lax.ppermute(near_rows, "gen", [(i, i ^ 1) for i in range(gen_count)])
    (load,) = call_once(
        load_kernel,
        [(real_count, share + EXTRA, NUM_BINS)],
        near_rows, far_rows, own, front_sums, back_sums,
    )
    rows_near, load = lax.optimization_barrier((real_rows, load))
    hall = trade(load, "real")
    front = near_rows_of(rows_near, real_rows.shape[0] // 8, 1)
    hall, front = lax.optimization_barrier((hall, front))
    grad_part = pair_sums(
        hall, near_rows, far_rows, front, real_rows, front_sq, back_sq, total_flows, total_real, 256
    )
    (grad_own,) = call_once(sum_kernel, [grad_part.shape], trade(grad_part, "real"))
    part = back_steps(trade(grad_own, "real"), val, sig, hidden)
    grad = swap_sum(part, "gen", gen_count, ((1,), (2,), (4, 8, 12)))
    (square,) = call_once(square_kernel, [(real_count, 8, 128)], grad)
    update, loss = pl.pallas_call(
        scale_kernel,
        grid=(1,),
        out_shape=[
            jax.ShapeDtypeStruct((local_steps, width), f32),
            jax.ShapeDtypeStruct((1,), f32),
        ],
        in_specs=[fixed(grad.shape), fixed(square.shape)],
        out_specs=[fixed((local_steps, width)), pl.BlockSpec(memory_space=SMEM)],
        compiler_params=params(),
    )(grad, trade(square, "real"))
    return (update.T, loss.reshape(()))


def solution(mesh):
    in_specs = (P("gen", None), P(None, "real"), P("gen"), P("real", None))
    out_specs = (P(None, "real"), P())
    body = functools.partial(per_device, mesh.shape["real"], mesh.shape["gen"])
    return jax.shard_map(
        body, mesh=mesh, in_specs=in_specs, out_specs=out_specs, check_vma=False
    )
```

```python
import functools
import math

import jax
import jax.numpy as jnp
from jax import lax
from jax.experimental import pallas as pl
from jax.experimental.pallas import tpu as pltpu
from jax.sharding import PartitionSpec as P

NUM_BINS = 256
SEQ_STEPS = 512
HID_WIDTH = 256
SPACING = 6.0 / NUM_BINS
LOG2E = math.log2(math.e)
UNIT = math.sqrt(LOG2E / 2.0) / SPACING
STEP = UNIT * SPACING
FAR = 1.0e6
EXTRA = 8
ROOT_2 = math.sqrt(1.0 / 2.0)
ROOT_8 = math.sqrt(1.0 / 8.0)

highest = lax.Precision.HIGHEST
f32 = jnp.float32
bf16 = jnp.bfloat16
NT = (((1,), (1,)), ((), ()))
NN = (((1,), (0,)), ((), ()))
VMEM = pltpu.VMEM
SMEM = pltpu.SMEM


def params(limit=48 << 20):
    return pltpu.CompilerParams(vmem_limit_bytes=limit)


def whole():
    return pl.BlockSpec(memory_space=VMEM)


def fixed(shape):
    return pl.BlockSpec(shape, lambda i: (0,) * len(shape))


def call_once(kernel, outs, *args, scalars=0, limit=48 << 20):
    return pl.pallas_call(
        kernel,
        grid=(1,),
        out_shape=[jax.ShapeDtypeStruct(s, f32) for s in outs],
        in_specs=[
            pl.BlockSpec(memory_space=SMEM) if i < scalars else fixed(a.shape)
            for i, a in enumerate(args)
        ],
        out_specs=[fixed(s) for s in outs],
        compiler_params=params(limit),
    )(*args)


def split(x):
    hi = x.astype(bf16)
    return hi, (x - hi.astype(f32)).astype(bf16)


def dot(a, b, dims):
    return lax.dot_general(a, b, dims, preferred_element_type=f32)


def count_kernel(first_ref, wt_ref, hid_ref, len_ref, out_ref, val_ref, sig_ref):
    pre = lax.dot_general(
        wt_ref[...], hid_ref[...], NT, precision=highest, preferred_element_type=f32
    )
    small = jnp.exp(-jnp.abs(pre))
    steps = jnp.maximum(pre, 0.0) + jnp.log1p(small)
    at = first_ref[0] + lax.broadcasted_iota(jnp.int32, pre.shape, 0)
    lens = len_ref[...]
    val = jnp.where(at < lens, steps * UNIT, FAR)
    val_ref[...] = val
    sig = 1.0 / (1.0 + jnp.exp(-pre))
    sig_ref[...] = sig / (lens.astype(f32) * (UNIT * SPACING * SPACING))

    def bins(i, carry):
        base = (8 * i).astype(f32) + 0.5
        rows = []
        for j in range(8):
            off = (base + j) * STEP - val
            e = jnp.exp2(-(off * off))
            rows.append(jnp.sum(e, 0, keepdims=True))
        out_ref[pl.ds(pl.multiple_of(8 * i, 8), 8), :] = jnp.concatenate(rows, 0)
        return carry

    lax.fori_loop(0, NUM_BINS // 8, bins, 0)
    out_ref[...] = out_ref[...].T


def back_kernel(gh_ref, val_ref, sig_ref, hid_ref, out_ref, ght_ref):
    parts, share = gh_ref.shape[0], gh_ref.shape[1] - EXTRA
    tall = val_ref.shape[0]
    gh = jnp.concatenate([gh_ref[p, :share, :] for p in range(parts)], 0)
    ght_ref[...] = gh.T
    val = val_ref[...]

    def bins(i, acc):
        base = (8 * i).astype(f32) + 0.5
        rows = ght_ref[pl.ds(pl.multiple_of(8 * i, 8), 8), :]
        for j in range(8):
            off = (base + j) * STEP - val
            e = jnp.exp2(-(off * off))
            acc = acc + (e * off) * rows[j : j + 1, :]
        return acc

    slope = lax.fori_loop(0, NUM_BINS // 8, bins, jnp.zeros_like(val))
    out_ref[0:tall, :] = lax.dot_general(
        slope * sig_ref[...], hid_ref[...], NN, precision=highest, preferred_element_type=f32
    )
    out_ref[tall:, :] = gh_ref[0, share:, :]


def back_steps(gh, val, sig, hidden):
    t, g = val.shape
    z = hidden.shape[1]
    return pl.pallas_call(
        back_kernel,
        grid=(1,),
        out_shape=jax.ShapeDtypeStruct((t + EXTRA, z), f32),
        in_specs=[fixed(gh.shape), fixed((t, g)), fixed((t, g)), fixed((g, z))],
        out_specs=fixed((t + EXTRA, z)),
        scratch_shapes=[VMEM((NUM_BINS, g), f32)],
        compiler_params=params(),
    )(gh, val, sig, hidden)


def row_squares(squares):
    hi, lo = split(squares)
    ones = jnp.ones((8, 2 * squares.shape[1]), bf16)
    return dot(ones, jnp.concatenate([hi, lo], 1), NT)


def stat_kernel(rows_ref, sum_ref, sq_ref, *near_refs):
    rows = rows_ref[...]
    w = rows.shape[1]
    near = rows.astype(bf16)
    for ref in near_refs:

        @pl.when(pl.program_id(0) == 0)
        def _():
            ref[...] = near[: ref.shape[0]]

    near = near.astype(f32)
    near = near * near
    half = w // 2
    sq_ref[...] = row_squares(near[:, :half] + near[:, half:])
    part = jnp.concatenate(
        [
            jnp.sum(rows.reshape(-1, 8, w), 0),
            jnp.sum((rows * rows).reshape(-1, 8, w), 0),
        ],
        0,
    )

    @pl.when(pl.program_id(0) == 0)
    def _():
        sum_ref[...] = part

    @pl.when(pl.program_id(0) > 0)
    def _():
        sum_ref[...] += part


def row_stats(rows, block, start, count, near=0):
    w = rows.shape[1]
    extra = [near] if near else []
    return pl.pallas_call(
        stat_kernel,
        grid=(count,),
        out_shape=[
            jax.ShapeDtypeStruct((16, w), f32),
            jax.ShapeDtypeStruct((8, count * block), f32),
        ]
        + [jax.ShapeDtypeStruct((n, w), bf16) for n in extra],
        in_specs=[pl.BlockSpec((block, w), lambda i: (start + i, 0))],
        out_specs=[
            fixed((16, w)),
            pl.BlockSpec((8, block), lambda i: (0, i)),
        ]
        + [fixed((n, w)) for n in extra],
        compiler_params=params(),
        cost_estimate=pl.CostEstimate(
            flops=16 * count * block * w, bytes_accessed=4 * count * block * w, transcendentals=0
        ),
    )(rows)


def share_kernel(parts_ref, len_ref, out_ref):
    count = jnp.sum(parts_ref[...], 0)
    hist = count / len_ref[...].astype(f32)
    out_ref[...] = jnp.broadcast_to(hist[None], out_ref.shape)


def load_kernel(others_ref, more_ref, own_ref, front_ref, back_ref, out_ref):
    parts, share, w = others_ref.shape
    rows = jnp.concatenate(
        [r[...].reshape(parts * share, w) for r in (others_ref, more_ref)], 0
    )
    stats = jnp.concatenate(
        [
            jnp.sum(rows, 0, keepdims=True),
            jnp.sum(rows * rows, 0, keepdims=True),
            jnp.sum(front_ref[0:8, :] + back_ref[0:8, :], 0, keepdims=True),
            jnp.sum(front_ref[8:16, :] + back_ref[8:16, :], 0, keepdims=True),
            jnp.zeros((EXTRA - 4, w), f32),
        ],
        0,
    )
    load = jnp.concatenate([own_ref[0], stats], 0)
    out_ref[...] = jnp.broadcast_to(load[None], out_ref.shape)


def pair_kernel(
    cols, total_flows, total_real, hall_ref, others_ref, more_ref, front_ref, rows_ref,
    front_sq_ref, back_sq_ref, out_ref,
    rate_ref, h_ref, hc_ref, hs_ref, ip_ref, wh_ref, mat_ref, sum_ref, kacc_ref, held_ref, near_ref, sems,
):
    parts, tall, width = hall_ref.shape
    share = tall - EXTRA
    flows = parts * share
    front = front_ref.shape[0]
    rest = [
        pltpu.make_async_copy(
            rows_ref.at[pl.ds(at, at), :], held_ref.at[pl.ds(at - front, at), :], sems.at[c]
        )
        for c, at in enumerate((front, 2 * front, 4 * front))
    ]
    rest[0].start()
    rest[1].start()

    def prepare():
        h = jnp.concatenate([hall_ref[p, :share, :] for p in range(parts)], 0)
        h_ref[...] = h
        stats = hall_ref[0, share:, :]
        for p in range(1, parts):
            stats = stats + hall_ref[p, share:, :]
        line = (
            stats[1:2, :] / total_flows
            + stats[3:4, :] / total_real
            - 2.0 * ((stats[0:1, :] / total_flows) * (stats[2:3, :] / total_real))
        )
        spread = jnp.sum(line, 1, keepdims=True)
        rate = jnp.broadcast_to(LOG2E / (4.0 * spread), (8, 128))
        rate_ref[...] = rate
        one = rate[0:1, 0:1]
        hh, hl = split(h * (2.0 * one))
        hc_ref[...] = jnp.concatenate([hh, hl], 1)
        hs_ref[...] = jnp.broadcast_to(
            jnp.sum(h * h, 1, keepdims=True) * one - 1.0, hs_ref.shape
        )
        mat_ref[...] = jnp.zeros_like(mat_ref)
        sum_ref[...] = jnp.zeros_like(sum_ref)
        kacc_ref[...] = jnp.zeros_like(kacc_ref)

    prepare()
    rate = rate_ref[0:1, 0:1]

    def weigh(x, at, sums):
        a = jnp.exp2(x)
        a2 = a * a
        b = a2 * ROOT_2
        b = b * b
        c = b * 0.5
        c = c * c
        d = c * ROOT_8
        d = d * d
        w = (a + a2) + (b + c) + d

        def fold(v):
            t = v[:, 0:128]
            for q in range(1, v.shape[1] // 128):
                t = t + v[:, 128 * q : 128 * q + 128]
            return t

        sum_ref[at, :] += fold(w)
        out = []
        for v, total in zip((a2, b, c, d), sums):
            t = fold(v)
            for q in range(t.shape[0] // 8):
                total = total + t[8 * q : 8 * q + 8]
            out.append(total)
        return w, tuple(out)

    early = front // cols

    def first(p):
        if p < early:
            r = front_ref[p * cols : (p + 1) * cols, :]
        else:
            r = held_ref[(p - early) * cols : (p - early + 1) * cols, :].astype(bf16)
            near_ref[p % 3] = r
        ip_ref[p % 2] = dot(hc_ref[...], jnp.concatenate([r, r], 1), NT)

    def second(p, sums):
        ref, q = (front_sq_ref, p) if p < 4 * early else (back_sq_ref, p - 4 * early)
        sq = ref[0:1, q * cols : (q + 1) * cols] * rate
        for c in range(flows // 16):
            at = slice(16 * c, 16 * c + 16)
            x = (ip_ref[p % 2, at, :] - sq) - jnp.tile(hs_ref[at, :], (1, cols // 128))
            w, sums = weigh(x, at, sums)
            wh_ref[p % 2, at, :] = w.astype(bf16)
        return sums

    def third(p):
        if p < early:
            r = front_ref[p * cols : (p + 1) * cols, :]
        else:
            r = near_ref[p % 3]
        mat_ref[...] += dot(wh_ref[p % 2], r, NN)

    def keep(sums):
        for q in range(4):
            kacc_ref[8 * q : 8 * q + 8, :] += sums[q]

    zeros = (jnp.zeros((8, 128), f32),) * 4
    count = early + held_ref.shape[0] // cols
    sums = zeros
    first(0)
    for p in range(count):
        if p + 1 == early:
            rest[0].wait()
            rest[2].start()
        if p + 1 == 2 * early:
            rest[1].wait()
        if p + 1 == 4 * early:
            rest[2].wait()
        if p + 1 < count:
            first(p + 1)
        sums = second(p, sums)
        if p % 16 == 15:
            keep(sums)
            sums = zeros
        if p > 0:
            third(p - 1)
    third(count - 1)
    keep(sums)

    def complete():
        h = h_ref[...]

        def finish(scale):
            total = jnp.sum(sum_ref[...], 1, keepdims=True)
            grad = (total * h - mat_ref[...]) * (rate * (0.5 * scale))
            lanes = 0.5 * jnp.sum(sum_ref[...], 0, keepdims=True)
            for q, part in enumerate((1 / 4, 3 / 8, 7 / 16, 15 / 32)):
                lanes = lanes - part * jnp.sum(kacc_ref[8 * q : 8 * q + 8, :], 0, keepdims=True)
            return grad, jnp.sum(lanes, 1, keepdims=True)

        cross_g, cross_k = finish(4.0 / (total_real * LOG2E))
        mat_ref[...] = jnp.zeros_like(mat_ref)
        sum_ref[...] = jnp.zeros_like(sum_ref)
        kacc_ref[...] = jnp.zeros_like(kacc_ref)
        sums = zeros
        rows_all = jnp.concatenate(
            [r[...].reshape(-1, width) for r in (others_ref, more_ref)], 0
        )
        for p in range(rows_all.shape[0] // cols):
            rows = rows_all[p * cols : (p + 1) * cols]
            rh, rl = split(rows)
            hc = hc_ref[...]
            ip_ref[0] = dot(
                jnp.concatenate([hc, hc[:, :width]], 1),
                jnp.concatenate([rh, rh, rl], 1),
                NT,
            )
            sq = row_squares(rows * rows)[0:1, :] * rate
            for c in range(flows // 16):
                at = slice(16 * c, 16 * c + 16)
                x = (ip_ref[0, at, :] - sq) - jnp.tile(hs_ref[at, :], (1, cols // 128))
                w, sums = weigh(x, at, sums)
                wh, wl = split(w)
                wh_ref[0, at, :] = wh
                wh_ref[1, at, :] = wl
            wh, wl = wh_ref[0], wh_ref[1]
            mat_ref[...] += dot(
                jnp.concatenate([wh, wl, wh], 1), jnp.concatenate([rh, rh, rl], 0), NN
            )
        keep(sums)
        pair_g, pair_k = finish(-4.0 / (total_flows * LOG2E))
        grad = cross_g + pair_g
        loss = pair_k / (float(total_flows) * total_flows) - 2.0 * cross_k / (
            float(total_flows) * total_real
        )
        line = jnp.broadcast_to(loss, (EXTRA, width))
        for p in range(parts):
            out_ref[p, :share, :] = grad[p * share : (p + 1) * share]
            out_ref[p, share:, :] = line

    complete()


def pair_sums(hall, others, more, front, rows, front_sq, back_sq, total_flows, total_real, cols):
    n, w = rows.shape
    flows = hall.shape[0] * (hall.shape[1] - EXTRA)
    return pl.pallas_call(
        functools.partial(pair_kernel, cols, total_flows, total_real),
        grid=(1,),
        out_shape=jax.ShapeDtypeStruct(hall.shape, f32),
        in_specs=[
            fixed(hall.shape),
            fixed(others.shape),
            fixed(more.shape),
            whole(),
            pl.BlockSpec(memory_space=pl.ANY),
            fixed(front_sq.shape),
            fixed(back_sq.shape),
        ],
        out_specs=fixed(hall.shape),
        scratch_shapes=[
            VMEM((8, 128), f32),
            VMEM((flows, w), f32),
            VMEM((flows, 2 * w), bf16),
            VMEM((flows, 128), f32),
            VMEM((2, flows, cols), f32),
            VMEM((2, flows, cols), bf16),
            VMEM((flows, w), f32),
            VMEM((flows, 128), f32),
            VMEM((32, 128), f32),
            VMEM((n - front.shape[0], w), f32),
            VMEM((3, cols, w), bf16),
            pltpu.SemaphoreType.DMA((3,)),
        ],
        compiler_params=params(),
        cost_estimate=pl.CostEstimate(
            flops=6 * n * w * flows, bytes_accessed=4 * n * w, transcendentals=n * flows
        ),
    )(hall, others, more, front, rows, front_sq, back_sq)


def sum_kernel(parts_ref, out_ref):
    out_ref[...] = jnp.broadcast_to(jnp.sum(parts_ref[...], 0)[None], out_ref.shape)


def square_kernel(grad_ref, out_ref):
    grad = grad_ref[0 : grad_ref.shape[0] - EXTRA, :]
    lanes = jnp.sum(grad * grad, 0, keepdims=True)
    out_ref[...] = jnp.broadcast_to(jnp.sum(lanes, 1, keepdims=True)[None], out_ref.shape)


def scale_kernel(grad_ref, sq_ref, out_ref, loss_ref):
    mean_sq = jnp.sum(sq_ref[...], 0)[0:1, 0:1] * (1.0 / (HID_WIDTH * SEQ_STEPS))
    tall = out_ref.shape[0]
    out_ref[...] = grad_ref[0:tall, :] / jnp.sqrt(mean_sq + 1e-06)
    loss_ref[0] = jnp.max(grad_ref[tall : tall + 1, 0:128])


def swap_sum(x, axis, count, groups):
    for hops in groups:
        sent = [lax.ppermute(x, axis, [(i, i ^ hop) for i in range(count)]) for hop in hops]
        for other in sent:
            x = x + other
    return x


def trade(x, axis, groups=None):
    return lax.all_to_all(x, axis, 0, 0, axis_index_groups=groups, tiled=True)


def per_device(real_count, gen_count, hidden, weight, lengths, real_rows):
    real_index = lax.axis_index("real")
    flows, width = hidden.shape
    local_steps = weight.shape[1]
    total_flows = flows * gen_count
    total_real = real_rows.shape[0] * real_count
    share = flows // real_count
    block = min(4096, real_rows.shape[0] // 2)
    half = real_rows.shape[0] // block // 2
    first = jnp.full((1,), real_index * local_steps, jnp.int32)
    counts, val, sig = call_once(
        count_kernel,
        [(flows, NUM_BINS), (local_steps, flows), (local_steps, flows)],
        first, weight.T, hidden, lengths[None, :], scalars=1, limit=60 << 20,
    )
    rows_early, counts = lax.optimization_barrier((real_rows, counts))
    parts = trade(counts.reshape(real_count, share, NUM_BINS), "real")
    front_sums, front_sq, front = row_stats(
        rows_early, block, 0, half, real_rows.shape[0] // 8
    )
    own_len = lax.dynamic_slice_in_dim(lengths, real_index * share, share)[:, None]
    own_len, front_sums = lax.optimization_barrier((own_len, front_sums))
    (own,) = call_once(share_kernel, [(gen_count // 2, share, NUM_BINS)], parts, own_len)
    same = [list(range(c, gen_count, 2)) for c in range(2)]
    rows_late, own = lax.optimization_barrier((real_rows, own))
    near_rows = trade(own, "gen", same)
    back_sums, back_sq = row_stats(rows_late, block, half, half)
    near_rows, back_sums = lax.optimization_barrier((near_rows, back_sums))
    far_rows = lax.ppermute(near_rows, "gen", [(i, i ^ 1) for i in range(gen_count)])
    (load,) = call_once(
        load_kernel,
        [(real_count, share + EXTRA, NUM_BINS)],
        near_rows, far_rows, own, front_sums, back_sums,
    )
    hall = trade(load, "real")
    grad_part = pair_sums(
        hall, near_rows, far_rows, front, real_rows, front_sq, back_sq, total_flows, total_real, 256
    )
    (grad_own,) = call_once(sum_kernel, [grad_part.shape], trade(grad_part, "real"))
    part = back_steps(trade(grad_own, "real"), val, sig, hidden)
    grad = swap_sum(part, "gen", gen_count, ((1,), (2,), (4, 8, 12)))
    (square,) = call_once(square_kernel, [(real_count, 8, 128)], grad)
    update, loss = pl.pallas_call(
        scale_kernel,
        grid=(1,),
        out_shape=[
            jax.ShapeDtypeStruct((local_steps, width), f32),
            jax.ShapeDtypeStruct((1,), f32),
        ],
        in_specs=[fixed(grad.shape), fixed(square.shape)],
        out_specs=[fixed((local_steps, width)), pl.BlockSpec(memory_space=SMEM)],
        compiler_params=params(),
    )(grad, trade(square, "real"))
    return (update.T, loss.reshape(()))


def solution(mesh):
    in_specs = (P("gen", None), P(None, "real"), P("gen"), P("real", None))
    out_specs = (P(None, "real"), P())
    body = functools.partial(per_device, mesh.shape["real"], mesh.shape["gen"])
    return jax.shard_map(
        body, mesh=mesh, in_specs=in_specs, out_specs=out_specs, check_vma=False
    )
```

```python
import functools
import math

import jax
import jax.numpy as jnp
from jax import lax
from jax.experimental import pallas as pl
from jax.experimental.pallas import tpu as pltpu
from jax.sharding import PartitionSpec as P

NUM_BINS = 256
SEQ_STEPS = 512
HID_WIDTH = 256
SPACING = 6.0 / NUM_BINS
LOG2E = math.log2(math.e)
UNIT = math.sqrt(LOG2E / 2.0) / SPACING
STEP = UNIT * SPACING
FAR = 1.0e6
EXTRA = 8
TURN = 32
ROOT_2 = math.sqrt(1.0 / 2.0)
ROOT_8 = math.sqrt(1.0 / 8.0)

highest = lax.Precision.HIGHEST
f32 = jnp.float32
bf16 = jnp.bfloat16
NT = (((1,), (1,)), ((), ()))
NN = (((1,), (0,)), ((), ()))
VMEM = pltpu.VMEM
SMEM = pltpu.SMEM


def params(limit=48 << 20):
    return pltpu.CompilerParams(vmem_limit_bytes=limit)


def whole():
    return pl.BlockSpec(memory_space=VMEM)


def fixed(shape):
    return pl.BlockSpec(shape, lambda i: (0,) * len(shape))


def call_once(kernel, outs, *args, scalars=0, limit=48 << 20):
    return pl.pallas_call(
        kernel,
        grid=(1,),
        out_shape=[jax.ShapeDtypeStruct(s, f32) for s in outs],
        in_specs=[
            pl.BlockSpec(memory_space=SMEM) if i < scalars else fixed(a.shape)
            for i, a in enumerate(args)
        ],
        out_specs=[fixed(s) for s in outs],
        compiler_params=params(limit),
    )(*args)


def split(x):
    hi = x.astype(bf16)
    return hi, (x - hi.astype(f32)).astype(bf16)


def dot(a, b, dims):
    return lax.dot_general(a, b, dims, preferred_element_type=f32)


def count_kernel(first_ref, wt_ref, hid_ref, len_ref, out_ref, val_ref, sig_ref):
    pre = lax.dot_general(
        wt_ref[...], hid_ref[...], NT, precision=highest, preferred_element_type=f32
    )
    small = jnp.exp(-jnp.abs(pre))
    steps = jnp.maximum(pre, 0.0) + jnp.log1p(small)
    at = first_ref[0] + lax.broadcasted_iota(jnp.int32, pre.shape, 0)
    lens = len_ref[...]
    val = jnp.where(at < lens, steps * UNIT, FAR)
    val_ref[...] = val
    sig = 1.0 / (1.0 + jnp.exp(-pre))
    sig_ref[...] = sig / (lens.astype(f32) * (UNIT * SPACING * SPACING))

    def bins(i, carry):
        base = (TURN * i).astype(f32) + 0.5
        for k in range(0, TURN, 8):
            rows = []
            for j in range(k, k + 8):
                off = (base + j) * STEP - val
                e = jnp.exp2(-(off * off))
                rows.append(jnp.sum(e, 0, keepdims=True))
            at = pl.multiple_of(TURN * i + k, 8)
            out_ref[pl.ds(at, 8), :] = jnp.concatenate(rows, 0)
        return carry

    lax.fori_loop(0, NUM_BINS // TURN, bins, 0)
    out_ref[...] = out_ref[...].T


def back_kernel(gh_ref, val_ref, sig_ref, hid_ref, out_ref, ght_ref):
    parts, share = gh_ref.shape[0], gh_ref.shape[1] - EXTRA
    tall = val_ref.shape[0]
    gh = jnp.concatenate([gh_ref[p, :share, :] for p in range(parts)], 0)
    ght_ref[...] = gh.T
    val = val_ref[...]

    def bins(i, acc):
        base = (TURN * i).astype(f32) + 0.5
        rows = ght_ref[pl.ds(pl.multiple_of(TURN * i, TURN), TURN), :]
        for j in range(TURN):
            off = (base + j) * STEP - val
            e = jnp.exp2(-(off * off))
            acc = acc + (e * off) * rows[j : j + 1, :]
        return acc

    slope = lax.fori_loop(0, NUM_BINS // TURN, bins, jnp.zeros_like(val))
    out_ref[0:tall, :] = lax.dot_general(
        slope * sig_ref[...], hid_ref[...], NN, precision=highest, preferred_element_type=f32
    )
    out_ref[tall:, :] = gh_ref[0, share:, :]


def back_steps(gh, val, sig, hidden):
    t, g = val.shape
    z = hidden.shape[1]
    return pl.pallas_call(
        back_kernel,
        grid=(1,),
        out_shape=jax.ShapeDtypeStruct((t + EXTRA, z), f32),
        in_specs=[fixed(gh.shape), fixed((t, g)), fixed((t, g)), fixed((g, z))],
        out_specs=fixed((t + EXTRA, z)),
        scratch_shapes=[VMEM((NUM_BINS, g), f32)],
        compiler_params=params(),
    )(gh, val, sig, hidden)


def row_squares(squares):
    hi, lo = split(squares)
    ones = jnp.ones((8, 2 * squares.shape[1]), bf16)
    return dot(ones, jnp.concatenate([hi, lo], 1), NT)


def stat_kernel(rows_ref, sum_ref, sq_ref, *near_refs):
    rows = rows_ref[...]
    w = rows.shape[1]
    near = rows.astype(bf16)
    for ref in near_refs:

        @pl.when(pl.program_id(0) == 0)
        def _():
            ref[...] = near[: ref.shape[0]]

    near = near.astype(f32)
    near = near * near
    half = w // 2
    sq_ref[...] = row_squares(near[:, :half] + near[:, half:])
    part = jnp.concatenate(
        [
            jnp.sum(rows.reshape(-1, 8, w), 0),
            jnp.sum((rows * rows).reshape(-1, 8, w), 0),
        ],
        0,
    )

    @pl.when(pl.program_id(0) == 0)
    def _():
        sum_ref[...] = part

    @pl.when(pl.program_id(0) > 0)
    def _():
        sum_ref[...] += part


def row_stats(rows, block, start, count, near=0):
    w = rows.shape[1]
    extra = [near] if near else []
    return pl.pallas_call(
        stat_kernel,
        grid=(count,),
        out_shape=[
            jax.ShapeDtypeStruct((16, w), f32),
            jax.ShapeDtypeStruct((8, count * block), f32),
        ]
        + [jax.ShapeDtypeStruct((n, w), bf16) for n in extra],
        in_specs=[pl.BlockSpec((block, w), lambda i: (start + i, 0))],
        out_specs=[
            fixed((16, w)),
            pl.BlockSpec((8, block), lambda i: (0, i)),
        ]
        + [fixed((n, w)) for n in extra],
        compiler_params=params(),
        cost_estimate=pl.CostEstimate(
            flops=16 * count * block * w, bytes_accessed=4 * count * block * w, transcendentals=0
        ),
    )(rows)


def share_kernel(parts_ref, len_ref, out_ref):
    count = jnp.sum(parts_ref[...], 0)
    hist = count / len_ref[...].astype(f32)
    out_ref[...] = jnp.broadcast_to(hist[None], out_ref.shape)


def load_kernel(others_ref, more_ref, own_ref, front_ref, back_ref, out_ref):
    parts, share, w = others_ref.shape
    rows = jnp.concatenate(
        [r[...].reshape(parts * share, w) for r in (others_ref, more_ref)], 0
    )
    stats = jnp.concatenate(
        [
            jnp.sum(rows, 0, keepdims=True),
            jnp.sum(rows * rows, 0, keepdims=True),
            jnp.sum(front_ref[0:8, :] + back_ref[0:8, :], 0, keepdims=True),
            jnp.sum(front_ref[8:16, :] + back_ref[8:16, :], 0, keepdims=True),
            jnp.zeros((EXTRA - 4, w), f32),
        ],
        0,
    )
    load = jnp.concatenate([own_ref[0], stats], 0)
    out_ref[...] = jnp.broadcast_to(load[None], out_ref.shape)


def pair_kernel(
    cols, total_flows, total_real, hall_ref, others_ref, more_ref, front_ref, rows_ref,
    front_sq_ref, back_sq_ref, out_ref,
    rate_ref, h_ref, hc_ref, hs_ref, ip_ref, wh_ref, mat_ref, sum_ref, kacc_ref, held_ref, near_ref, sems,
):
    parts, tall, width = hall_ref.shape
    share = tall - EXTRA
    flows = parts * share
    front = front_ref.shape[0]
    rest = [
        pltpu.make_async_copy(
            rows_ref.at[pl.ds(at, at), :], held_ref.at[pl.ds(at - front, at), :], sems.at[c]
        )
        for c, at in enumerate((front, 2 * front, 4 * front))
    ]
    rest[0].start()
    rest[1].start()

    def prepare():
        h = jnp.concatenate([hall_ref[p, :share, :] for p in range(parts)], 0)
        h_ref[...] = h
        stats = hall_ref[0, share:, :]
        for p in range(1, parts):
            stats = stats + hall_ref[p, share:, :]
        line = (
            stats[1:2, :] / total_flows
            + stats[3:4, :] / total_real
            - 2.0 * ((stats[0:1, :] / total_flows) * (stats[2:3, :] / total_real))
        )
        spread = jnp.sum(line, 1, keepdims=True)
        rate = jnp.broadcast_to(LOG2E / (4.0 * spread), (8, 128))
        rate_ref[...] = rate
        one = rate[0:1, 0:1]
        hh, hl = split(h * (2.0 * one))
        hc_ref[...] = jnp.concatenate([hh, hl], 1)
        hs_ref[...] = jnp.broadcast_to(
            jnp.sum(h * h, 1, keepdims=True) * one - 1.0, hs_ref.shape
        )
        mat_ref[...] = jnp.zeros_like(mat_ref)
        sum_ref[...] = jnp.zeros_like(sum_ref)
        kacc_ref[...] = jnp.zeros_like(kacc_ref)

    prepare()
    rate = rate_ref[0:1, 0:1]

    def weigh(x, at, sums):
        a = jnp.exp2(x)
        a2 = a * a
        b = a2 * ROOT_2
        b = b * b
        c = b * 0.5
        c = c * c
        d = c * ROOT_8
        d = d * d
        w = (a + a2) + (b + c) + d

        def fold(v):
            t = v[:, 0:128]
            for q in range(1, v.shape[1] // 128):
                t = t + v[:, 128 * q : 128 * q + 128]
            return t

        sum_ref[at, :] += fold(w)
        out = []
        for v, total in zip((a2, b, c, d), sums):
            t = fold(v)
            for q in range(t.shape[0] // 8):
                total = total + t[8 * q : 8 * q + 8]
            out.append(total)
        return w, tuple(out)

    early = front // cols

    def first(p):
        if p < early:
            r = front_ref[p * cols : (p + 1) * cols, :]
        else:
            r = held_ref[(p - early) * cols : (p - early + 1) * cols, :].astype(bf16)
            near_ref[p % 3] = r
        ip_ref[p % 2] = dot(hc_ref[...], jnp.concatenate([r, r], 1), NT)

    def second(p, sums):
        ref, q = (front_sq_ref, p) if p < 4 * early else (back_sq_ref, p - 4 * early)
        sq = ref[0:1, q * cols : (q + 1) * cols] * rate
        for c in range(flows // 16):
            at = slice(16 * c, 16 * c + 16)
            x = (ip_ref[p % 2, at, :] - sq) - jnp.tile(hs_ref[at, :], (1, cols // 128))
            w, sums = weigh(x, at, sums)
            wh_ref[p % 2, at, :] = w.astype(bf16)
        return sums

    def third(p):
        if p < early:
            r = front_ref[p * cols : (p + 1) * cols, :]
        else:
            r = near_ref[p % 3]
        mat_ref[...] += dot(wh_ref[p % 2], r, NN)

    def keep(sums):
        for q in range(4):
            kacc_ref[8 * q : 8 * q + 8, :] += sums[q]

    zeros = (jnp.zeros((8, 128), f32),) * 4
    count = early + held_ref.shape[0] // cols
    sums = zeros
    first(0)
    for p in range(count):
        if p + 1 == early:
            rest[0].wait()
            rest[2].start()
        if p + 1 == 2 * early:
            rest[1].wait()
        if p + 1 == 4 * early:
            rest[2].wait()
        if p + 1 < count:
            first(p + 1)
        sums = second(p, sums)
        if p % 16 == 15:
            keep(sums)
            sums = zeros
        if p > 0:
            third(p - 1)
    third(count - 1)
    keep(sums)

    def complete():
        h = h_ref[...]

        def finish(scale):
            total = jnp.sum(sum_ref[...], 1, keepdims=True)
            grad = (total * h - mat_ref[...]) * (rate * (0.5 * scale))
            lanes = 0.5 * jnp.sum(sum_ref[...], 0, keepdims=True)
            for q, part in enumerate((1 / 4, 3 / 8, 7 / 16, 15 / 32)):
                lanes = lanes - part * jnp.sum(kacc_ref[8 * q : 8 * q + 8, :], 0, keepdims=True)
            return grad, jnp.sum(lanes, 1, keepdims=True)

        cross_g, cross_k = finish(4.0 / (total_real * LOG2E))
        mat_ref[...] = jnp.zeros_like(mat_ref)
        sum_ref[...] = jnp.zeros_like(sum_ref)
        kacc_ref[...] = jnp.zeros_like(kacc_ref)
        sums = zeros
        rows_all = jnp.concatenate(
            [r[...].reshape(-1, width) for r in (others_ref, more_ref)], 0
        )
        for p in range(rows_all.shape[0] // cols):
            rows = rows_all[p * cols : (p + 1) * cols]
            rh, rl = split(rows)
            hc = hc_ref[...]
            ip_ref[0] = dot(
                jnp.concatenate([hc, hc[:, :width]], 1),
                jnp.concatenate([rh, rh, rl], 1),
                NT,
            )
            sq = row_squares(rows * rows)[0:1, :] * rate
            for c in range(flows // 16):
                at = slice(16 * c, 16 * c + 16)
                x = (ip_ref[0, at, :] - sq) - jnp.tile(hs_ref[at, :], (1, cols // 128))
                w, sums = weigh(x, at, sums)
                wh, wl = split(w)
                wh_ref[0, at, :] = wh
                wh_ref[1, at, :] = wl
            wh, wl = wh_ref[0], wh_ref[1]
            mat_ref[...] += dot(
                jnp.concatenate([wh, wl, wh], 1), jnp.concatenate([rh, rh, rl], 0), NN
            )
        keep(sums)
        pair_g, pair_k = finish(-4.0 / (total_flows * LOG2E))
        grad = cross_g + pair_g
        loss = pair_k / (float(total_flows) * total_flows) - 2.0 * cross_k / (
            float(total_flows) * total_real
        )
        line = jnp.broadcast_to(loss, (EXTRA, width))
        for p in range(parts):
            out_ref[p, :share, :] = grad[p * share : (p + 1) * share]
            out_ref[p, share:, :] = line

    complete()


def pair_sums(hall, others, more, front, rows, front_sq, back_sq, total_flows, total_real, cols):
    n, w = rows.shape
    flows = hall.shape[0] * (hall.shape[1] - EXTRA)
    return pl.pallas_call(
        functools.partial(pair_kernel, cols, total_flows, total_real),
        grid=(1,),
        out_shape=jax.ShapeDtypeStruct(hall.shape, f32),
        in_specs=[
            fixed(hall.shape),
            fixed(others.shape),
            fixed(more.shape),
            whole(),
            pl.BlockSpec(memory_space=pl.ANY),
            fixed(front_sq.shape),
            fixed(back_sq.shape),
        ],
        out_specs=fixed(hall.shape),
        scratch_shapes=[
            VMEM((8, 128), f32),
            VMEM((flows, w), f32),
            VMEM((flows, 2 * w), bf16),
            VMEM((flows, 128), f32),
            VMEM((2, flows, cols), f32),
            VMEM((2, flows, cols), bf16),
            VMEM((flows, w), f32),
            VMEM((flows, 128), f32),
            VMEM((32, 128), f32),
            VMEM((n - front.shape[0], w), f32),
            VMEM((3, cols, w), bf16),
            pltpu.SemaphoreType.DMA((3,)),
        ],
        compiler_params=params(),
        cost_estimate=pl.CostEstimate(
            flops=6 * n * w * flows, bytes_accessed=4 * n * w, transcendentals=n * flows
        ),
    )(hall, others, more, front, rows, front_sq, back_sq)


def sum_kernel(parts_ref, out_ref):
    out_ref[...] = jnp.broadcast_to(jnp.sum(parts_ref[...], 0)[None], out_ref.shape)


def square_kernel(grad_ref, out_ref):
    grad = grad_ref[0 : grad_ref.shape[0] - EXTRA, :]
    lanes = jnp.sum(grad * grad, 0, keepdims=True)
    out_ref[...] = jnp.broadcast_to(jnp.sum(lanes, 1, keepdims=True)[None], out_ref.shape)


def scale_kernel(grad_ref, sq_ref, out_ref, loss_ref):
    mean_sq = jnp.sum(sq_ref[...], 0)[0:1, 0:1] * (1.0 / (HID_WIDTH * SEQ_STEPS))
    tall = out_ref.shape[0]
    out_ref[...] = grad_ref[0:tall, :] / jnp.sqrt(mean_sq + 1e-06)
    loss_ref[0] = jnp.max(grad_ref[tall : tall + 1, 0:128])


def swap_sum(x, axis, count, groups):
    for hops in groups:
        sent = [lax.ppermute(x, axis, [(i, i ^ hop) for i in range(count)]) for hop in hops]
        for other in sent:
            x = x + other
    return x


def trade(x, axis, groups=None):
    return lax.all_to_all(x, axis, 0, 0, axis_index_groups=groups, tiled=True)


def per_device(real_count, gen_count, hidden, weight, lengths, real_rows):
    real_index = lax.axis_index("real")
    flows, width = hidden.shape
    local_steps = weight.shape[1]
    total_flows = flows * gen_count
    total_real = real_rows.shape[0] * real_count
    share = flows // real_count
    block = min(4096, real_rows.shape[0] // 2)
    half = real_rows.shape[0] // block // 2
    first = jnp.full((1,), real_index * local_steps, jnp.int32)
    counts, val, sig = call_once(
        count_kernel,
        [(flows, NUM_BINS), (local_steps, flows), (local_steps, flows)],
        first, weight.T, hidden, lengths[None, :], scalars=1, limit=60 << 20,
    )
    rows_early, counts = lax.optimization_barrier((real_rows, counts))
    parts = trade(counts.reshape(real_count, share, NUM_BINS), "real")
    front_sums, front_sq, front = row_stats(
        rows_early, block, 0, half, real_rows.shape[0] // 8
    )
    own_len = lax.dynamic_slice_in_dim(lengths, real_index * share, share)[:, None]
    own_len, front_sums = lax.optimization_barrier((own_len, front_sums))
    (own,) = call_once(share_kernel, [(gen_count // 2, share, NUM_BINS)], parts, own_len)
    same = [list(range(c, gen_count, 2)) for c in range(2)]
    rows_late, own = lax.optimization_barrier((real_rows, own))
    near_rows = trade(own, "gen", same)
    back_sums, back_sq = row_stats(rows_late, block, half, half)
    near_rows, back_sums = lax.optimization_barrier((near_rows, back_sums))
    far_rows = lax.ppermute(near_rows, "gen", [(i, i ^ 1) for i in range(gen_count)])
    (load,) = call_once(
        load_kernel,
        [(real_count, share + EXTRA, NUM_BINS)],
        near_rows, far_rows, own, front_sums, back_sums,
    )
    hall = trade(load, "real")
    grad_part = pair_sums(
        hall, near_rows, far_rows, front, real_rows, front_sq, back_sq, total_flows, total_real, 256
    )
    (grad_own,) = call_once(sum_kernel, [grad_part.shape], trade(grad_part, "real"))
    part = back_steps(trade(grad_own, "real"), val, sig, hidden)
    grad = swap_sum(part, "gen", gen_count, ((1,), (2,), (4, 8, 12)))
    (square,) = call_once(square_kernel, [(real_count, 8, 128)], grad)
    update, loss = pl.pallas_call(
        scale_kernel,
        grid=(1,),
        out_shape=[
            jax.ShapeDtypeStruct((local_steps, width), f32),
            jax.ShapeDtypeStruct((1,), f32),
        ],
        in_specs=[fixed(grad.shape), fixed(square.shape)],
        out_specs=[fixed((local_steps, width)), pl.BlockSpec(memory_space=SMEM)],
        compiler_params=params(),
    )(grad, trade(square, "real"))
    return (update.T, loss.reshape(()))


def solution(mesh):
    in_specs = (P("gen", None), P(None, "real"), P("gen"), P("real", None))
    out_specs = (P(None, "real"), P())
    body = functools.partial(per_device, mesh.shape["real"], mesh.shape["gen"])
    return jax.shard_map(
        body, mesh=mesh, in_specs=in_specs, out_specs=out_specs, check_vma=False
    )
```

```python
import functools
import math

import jax
import jax.numpy as jnp
from jax import lax
from jax.experimental import pallas as pl
from jax.experimental.pallas import tpu as pltpu
from jax.sharding import PartitionSpec as P

NUM_BINS = 256
SEQ_STEPS = 512
HID_WIDTH = 256
SPACING = 6.0 / NUM_BINS
LOG2E = math.log2(math.e)
UNIT = math.sqrt(LOG2E / 2.0) / SPACING
STEP = UNIT * SPACING
FAR = 1.0e6
EXTRA = 8
TURN = 64
ROOT_2 = math.sqrt(1.0 / 2.0)
ROOT_8 = math.sqrt(1.0 / 8.0)

highest = lax.Precision.HIGHEST
f32 = jnp.float32
bf16 = jnp.bfloat16
NT = (((1,), (1,)), ((), ()))
NN = (((1,), (0,)), ((), ()))
VMEM = pltpu.VMEM
SMEM = pltpu.SMEM


def params(limit=48 << 20):
    return pltpu.CompilerParams(vmem_limit_bytes=limit)


def whole():
    return pl.BlockSpec(memory_space=VMEM)


def fixed(shape):
    return pl.BlockSpec(shape, lambda i: (0,) * len(shape))


def call_once(kernel, outs, *args, scalars=0, limit=48 << 20):
    return pl.pallas_call(
        kernel,
        grid=(1,),
        out_shape=[jax.ShapeDtypeStruct(s, f32) for s in outs],
        in_specs=[
            pl.BlockSpec(memory_space=SMEM) if i < scalars else fixed(a.shape)
            for i, a in enumerate(args)
        ],
        out_specs=[fixed(s) for s in outs],
        compiler_params=params(limit),
    )(*args)


def split(x):
    hi = x.astype(bf16)
    return hi, (x - hi.astype(f32)).astype(bf16)


def dot(a, b, dims):
    return lax.dot_general(a, b, dims, preferred_element_type=f32)


def count_kernel(first_ref, wt_ref, hid_ref, len_ref, out_ref, val_ref, sig_ref):
    pre = lax.dot_general(
        wt_ref[...], hid_ref[...], NT, precision=highest, preferred_element_type=f32
    )
    small = jnp.exp(-jnp.abs(pre))
    steps = jnp.maximum(pre, 0.0) + jnp.log1p(small)
    at = first_ref[0] + lax.broadcasted_iota(jnp.int32, pre.shape, 0)
    lens = len_ref[...]
    val = jnp.where(at < lens, steps * UNIT, FAR)
    val_ref[...] = val
    sig = 1.0 / (1.0 + jnp.exp(-pre))
    sig_ref[...] = sig / (lens.astype(f32) * (UNIT * SPACING * SPACING))

    def bins(i, carry):
        base = (TURN * i).astype(f32) + 0.5
        for k in range(0, TURN, 8):
            rows = []
            for j in range(k, k + 8):
                off = (base + j) * STEP - val
                e = jnp.exp2(-(off * off))
                rows.append(jnp.sum(e, 0, keepdims=True))
            at = pl.multiple_of(TURN * i + k, 8)
            out_ref[pl.ds(at, 8), :] = jnp.concatenate(rows, 0)
        return carry

    lax.fori_loop(0, NUM_BINS // TURN, bins, 0)
    out_ref[...] = out_ref[...].T


def back_kernel(gh_ref, val_ref, sig_ref, hid_ref, out_ref, ght_ref):
    parts, share = gh_ref.shape[0], gh_ref.shape[1] - EXTRA
    tall = val_ref.shape[0]
    gh = jnp.concatenate([gh_ref[p, :share, :] for p in range(parts)], 0)
    ght_ref[...] = gh.T
    val = val_ref[...]

    def bins(i, acc):
        base = (TURN * i).astype(f32) + 0.5
        rows = ght_ref[pl.ds(pl.multiple_of(TURN * i, TURN), TURN), :]
        for j in range(TURN):
            off = (base + j) * STEP - val
            e = jnp.exp2(-(off * off))
            acc = acc + (e * off) * rows[j : j + 1, :]
        return acc

    slope = lax.fori_loop(0, NUM_BINS // TURN, bins, jnp.zeros_like(val))
    out_ref[0:tall, :] = lax.dot_general(
        slope * sig_ref[...], hid_ref[...], NN, precision=highest, preferred_element_type=f32
    )
    out_ref[tall:, :] = gh_ref[0, share:, :]


def back_steps(gh, val, sig, hidden):
    t, g = val.shape
    z = hidden.shape[1]
    return pl.pallas_call(
        back_kernel,
        grid=(1,),
        out_shape=jax.ShapeDtypeStruct((t + EXTRA, z), f32),
        in_specs=[whole()] * 4,
        out_specs=whole(),
        scratch_shapes=[VMEM((NUM_BINS, g), f32)],
        compiler_params=params(),
    )(gh, val, sig, hidden)


def row_squares(squares):
    hi, lo = split(squares)
    ones = jnp.ones((8, 2 * squares.shape[1]), bf16)
    return dot(ones, jnp.concatenate([hi, lo], 1), NT)


def stat_kernel(rows_ref, sum_ref, sq_ref, *near_refs):
    rows = rows_ref[...]
    w = rows.shape[1]
    near = rows.astype(bf16)
    for ref in near_refs:

        @pl.when(pl.program_id(0) == 0)
        def _():
            ref[...] = near[: ref.shape[0]]

    near = near.astype(f32)
    near = near * near
    half = w // 2
    sq_ref[...] = row_squares(near[:, :half] + near[:, half:])
    part = jnp.concatenate(
        [
            jnp.sum(rows.reshape(-1, 8, w), 0),
            jnp.sum((rows * rows).reshape(-1, 8, w), 0),
        ],
        0,
    )

    @pl.when(pl.program_id(0) == 0)
    def _():
        sum_ref[...] = part

    @pl.when(pl.program_id(0) > 0)
    def _():
        sum_ref[...] += part


def row_stats(rows, block, start, count, near=0):
    w = rows.shape[1]
    extra = [near] if near else []
    return pl.pallas_call(
        stat_kernel,
        grid=(count,),
        out_shape=[
            jax.ShapeDtypeStruct((16, w), f32),
            jax.ShapeDtypeStruct((8, count * block), f32),
        ]
        + [jax.ShapeDtypeStruct((n, w), bf16) for n in extra],
        in_specs=[pl.BlockSpec((block, w), lambda i: (start + i, 0))],
        out_specs=[
            fixed((16, w)),
            pl.BlockSpec((8, block), lambda i: (0, i)),
        ]
        + [fixed((n, w)) for n in extra],
        compiler_params=params(),
        cost_estimate=pl.CostEstimate(
            flops=16 * count * block * w, bytes_accessed=4 * count * block * w, transcendentals=0
        ),
    )(rows)


def share_kernel(parts_ref, len_ref, out_ref):
    count = jnp.sum(parts_ref[...], 0)
    hist = count / len_ref[...].astype(f32)
    out_ref[...] = jnp.broadcast_to(hist[None], out_ref.shape)


def load_kernel(others_ref, more_ref, own_ref, front_ref, back_ref, out_ref):
    parts, share, w = others_ref.shape
    rows = jnp.concatenate(
        [r[...].reshape(parts * share, w) for r in (others_ref, more_ref)], 0
    )
    stats = jnp.concatenate(
        [
            jnp.sum(rows, 0, keepdims=True),
            jnp.sum(rows * rows, 0, keepdims=True),
            jnp.sum(front_ref[0:8, :] + back_ref[0:8, :], 0, keepdims=True),
            jnp.sum(front_ref[8:16, :] + back_ref[8:16, :], 0, keepdims=True),
            jnp.zeros((EXTRA - 4, w), f32),
        ],
        0,
    )
    load = jnp.concatenate([own_ref[0], stats], 0)
    out_ref[...] = jnp.broadcast_to(load[None], out_ref.shape)


def pair_kernel(
    cols, total_flows, total_real, hall_ref, others_ref, more_ref, front_ref, rows_ref,
    front_sq_ref, back_sq_ref, out_ref,
    rate_ref, h_ref, hc_ref, hs_ref, ip_ref, wh_ref, mat_ref, sum_ref, kacc_ref, held_ref, near_ref, sems,
):
    parts, tall, width = hall_ref.shape
    share = tall - EXTRA
    flows = parts * share
    front = front_ref.shape[0]
    rest = [
        pltpu.make_async_copy(
            rows_ref.at[pl.ds(at, at), :], held_ref.at[pl.ds(at - front, at), :], sems.at[c]
        )
        for c, at in enumerate((front, 2 * front, 4 * front))
    ]
    rest[0].start()
    rest[1].start()

    def prepare():
        h = jnp.concatenate([hall_ref[p, :share, :] for p in range(parts)], 0)
        h_ref[...] = h
        stats = hall_ref[0, share:, :]
        for p in range(1, parts):
            stats = stats + hall_ref[p, share:, :]
        line = (
            stats[1:2, :] / total_flows
            + stats[3:4, :] / total_real
            - 2.0 * ((stats[0:1, :] / total_flows) * (stats[2:3, :] / total_real))
        )
        spread = jnp.sum(line, 1, keepdims=True)
        rate = jnp.broadcast_to(LOG2E / (4.0 * spread), (8, 128))
        rate_ref[...] = rate
        one = rate[0:1, 0:1]
        hh, hl = split(h * (2.0 * one))
        hc_ref[...] = jnp.concatenate([hh, hl], 1)
        hs_ref[...] = jnp.broadcast_to(
            jnp.sum(h * h, 1, keepdims=True) * one - 1.0, hs_ref.shape
        )
        mat_ref[...] = jnp.zeros_like(mat_ref)
        sum_ref[...] = jnp.zeros_like(sum_ref)
        kacc_ref[...] = jnp.zeros_like(kacc_ref)

    prepare()
    rate = rate_ref[0:1, 0:1]

    def weigh(x, at, sums):
        a = jnp.exp2(x)
        a2 = a * a
        b = a2 * ROOT_2
        b = b * b
        c = b * 0.5
        c = c * c
        d = c * ROOT_8
        d = d * d
        w = (a + a2) + (b + c) + d

        def fold(v):
            t = v[:, 0:128]
            for q in range(1, v.shape[1] // 128):
                t = t + v[:, 128 * q : 128 * q + 128]
            return t

        sum_ref[at, :] += fold(w)
        out = []
        for v, total in zip((a2, b, c, d), sums):
            t = fold(v)
            for q in range(t.shape[0] // 8):
                total = total + t[8 * q : 8 * q + 8]
            out.append(total)
        return w, tuple(out)

    early = front // cols

    def first(p):
        if p < early:
            r = front_ref[p * cols : (p + 1) * cols, :]
        else:
            r = held_ref[(p - early) * cols : (p - early + 1) * cols, :].astype(bf16)
            near_ref[p % 3] = r
        ip_ref[p % 2] = dot(hc_ref[...], jnp.concatenate([r, r], 1), NT)

    def second(p, sums):
        ref, q = (front_sq_ref, p) if p < 4 * early else (back_sq_ref, p - 4 * early)
        sq = ref[0:1, q * cols : (q + 1) * cols] * rate
        for c in range(flows // 16):
            at = slice(16 * c, 16 * c + 16)
            x = (ip_ref[p % 2, at, :] - sq) - jnp.tile(hs_ref[at, :], (1, cols // 128))
            w, sums = weigh(x, at, sums)
            wh_ref[p % 2, at, :] = w.astype(bf16)
        return sums

    def third(p):
        if p < early:
            r = front_ref[p * cols : (p + 1) * cols, :]
        else:
            r = near_ref[p % 3]
        mat_ref[...] += dot(wh_ref[p % 2], r, NN)

    def keep(sums):
        for q in range(4):
            kacc_ref[8 * q : 8 * q + 8, :] += sums[q]

    zeros = (jnp.zeros((8, 128), f32),) * 4
    count = early + held_ref.shape[0] // cols
    sums = zeros
    first(0)
    for p in range(count):
        if p + 1 == early:
            rest[0].wait()
            rest[2].start()
        if p + 1 == 2 * early:
            rest[1].wait()
        if p + 1 == 4 * early:
            rest[2].wait()
        if p + 1 < count:
            first(p + 1)
        sums = second(p, sums)
        if p % 16 == 15:
            keep(sums)
            sums = zeros
        if p > 0:
            third(p - 1)
    third(count - 1)
    keep(sums)

    def complete():
        h = h_ref[...]

        def finish(scale):
            total = jnp.sum(sum_ref[...], 1, keepdims=True)
            grad = (total * h - mat_ref[...]) * (rate * (0.5 * scale))
            lanes = 0.5 * jnp.sum(sum_ref[...], 0, keepdims=True)
            for q, part in enumerate((1 / 4, 3 / 8, 7 / 16, 15 / 32)):
                lanes = lanes - part * jnp.sum(kacc_ref[8 * q : 8 * q + 8, :], 0, keepdims=True)
            return grad, jnp.sum(lanes, 1, keepdims=True)

        cross_g, cross_k = finish(4.0 / (total_real * LOG2E))
        mat_ref[...] = jnp.zeros_like(mat_ref)
        sum_ref[...] = jnp.zeros_like(sum_ref)
        kacc_ref[...] = jnp.zeros_like(kacc_ref)
        sums = zeros
        rows_all = jnp.concatenate(
            [r[...].reshape(-1, width) for r in (others_ref, more_ref)], 0
        )
        for p in range(rows_all.shape[0] // cols):
            rows = rows_all[p * cols : (p + 1) * cols]
            rh, rl = split(rows)
            hc = hc_ref[...]
            ip_ref[0] = dot(
                jnp.concatenate([hc, hc[:, :width]], 1),
                jnp.concatenate([rh, rh, rl], 1),
                NT,
            )
            sq = row_squares(rows * rows)[0:1, :] * rate
            for c in range(flows // 16):
                at = slice(16 * c, 16 * c + 16)
                x = (ip_ref[0, at, :] - sq) - jnp.tile(hs_ref[at, :], (1, cols // 128))
                w, sums = weigh(x, at, sums)
                wh, wl = split(w)
                wh_ref[0, at, :] = wh
                wh_ref[1, at, :] = wl
            wh, wl = wh_ref[0], wh_ref[1]
            mat_ref[...] += dot(
                jnp.concatenate([wh, wl, wh], 1), jnp.concatenate([rh, rh, rl], 0), NN
            )
        keep(sums)
        pair_g, pair_k = finish(-4.0 / (total_flows * LOG2E))
        grad = cross_g + pair_g
        loss = pair_k / (float(total_flows) * total_flows) - 2.0 * cross_k / (
            float(total_flows) * total_real
        )
        line = jnp.broadcast_to(loss, (EXTRA, width))
        for p in range(parts):
            out_ref[p, :share, :] = grad[p * share : (p + 1) * share]
            out_ref[p, share:, :] = line

    complete()


def pair_sums(hall, others, more, front, rows, front_sq, back_sq, total_flows, total_real, cols):
    n, w = rows.shape
    flows = hall.shape[0] * (hall.shape[1] - EXTRA)
    return pl.pallas_call(
        functools.partial(pair_kernel, cols, total_flows, total_real),
        grid=(1,),
        out_shape=jax.ShapeDtypeStruct(hall.shape, f32),
        in_specs=[
            fixed(hall.shape),
            fixed(others.shape),
            fixed(more.shape),
            whole(),
            pl.BlockSpec(memory_space=pl.ANY),
            fixed(front_sq.shape),
            fixed(back_sq.shape),
        ],
        out_specs=fixed(hall.shape),
        scratch_shapes=[
            VMEM((8, 128), f32),
            VMEM((flows, w), f32),
            VMEM((flows, 2 * w), bf16),
            VMEM((flows, 128), f32),
            VMEM((2, flows, cols), f32),
            VMEM((2, flows, cols), bf16),
            VMEM((flows, w), f32),
            VMEM((flows, 128), f32),
            VMEM((32, 128), f32),
            VMEM((n - front.shape[0], w), f32),
            VMEM((3, cols, w), bf16),
            pltpu.SemaphoreType.DMA((3,)),
        ],
        compiler_params=params(),
        cost_estimate=pl.CostEstimate(
            flops=6 * n * w * flows, bytes_accessed=4 * n * w, transcendentals=n * flows
        ),
    )(hall, others, more, front, rows, front_sq, back_sq)


def sum_kernel(parts_ref, out_ref):
    out_ref[...] = jnp.broadcast_to(jnp.sum(parts_ref[...], 0)[None], out_ref.shape)


def square_kernel(grad_ref, out_ref):
    grad = grad_ref[0 : grad_ref.shape[0] - EXTRA, :]
    lanes = jnp.sum(grad * grad, 0, keepdims=True)
    out_ref[...] = jnp.broadcast_to(jnp.sum(lanes, 1, keepdims=True)[None], out_ref.shape)


def scale_kernel(grad_ref, sq_ref, out_ref, loss_ref):
    mean_sq = jnp.sum(sq_ref[...], 0)[0:1, 0:1] * (1.0 / (HID_WIDTH * SEQ_STEPS))
    tall = out_ref.shape[0]
    out_ref[...] = grad_ref[0:tall, :] / jnp.sqrt(mean_sq + 1e-06)
    loss_ref[0] = jnp.max(grad_ref[tall : tall + 1, 0:128])


def swap_sum(x, axis, count, groups):
    for hops in groups:
        sent = [lax.ppermute(x, axis, [(i, i ^ hop) for i in range(count)]) for hop in hops]
        for other in sent:
            x = x + other
    return x


def trade(x, axis, groups=None):
    return lax.all_to_all(x, axis, 0, 0, axis_index_groups=groups, tiled=True)


def per_device(real_count, gen_count, hidden, weight, lengths, real_rows):
    real_index = lax.axis_index("real")
    flows, width = hidden.shape
    local_steps = weight.shape[1]
    total_flows = flows * gen_count
    total_real = real_rows.shape[0] * real_count
    share = flows // real_count
    block = min(4096, real_rows.shape[0] // 2)
    half = real_rows.shape[0] // block // 2
    first = jnp.full((1,), real_index * local_steps, jnp.int32)
    counts, val, sig = call_once(
        count_kernel,
        [(flows, NUM_BINS), (local_steps, flows), (local_steps, flows)],
        first, weight.T, hidden, lengths[None, :], scalars=1, limit=60 << 20,
    )
    rows_early, counts = lax.optimization_barrier((real_rows, counts))
    parts = trade(counts.reshape(real_count, share, NUM_BINS), "real")
    front_sums, front_sq, front = row_stats(
        rows_early, block, 0, half, real_rows.shape[0] // 8
    )
    own_len = lax.dynamic_slice_in_dim(lengths, real_index * share, share)[:, None]
    own_len, front_sums = lax.optimization_barrier((own_len, front_sums))
    (own,) = call_once(share_kernel, [(gen_count // 2, share, NUM_BINS)], parts, own_len)
    same = [list(range(c, gen_count, 2)) for c in range(2)]
    rows_late, own = lax.optimization_barrier((real_rows, own))
    near_rows = trade(own, "gen", same)
    back_sums, back_sq = row_stats(rows_late, block, half, half)
    near_rows, back_sums = lax.optimization_barrier((near_rows, back_sums))
    far_rows = lax.ppermute(near_rows, "gen", [(i, i ^ 1) for i in range(gen_count)])
    (load,) = call_once(
        load_kernel,
        [(real_count, share + EXTRA, NUM_BINS)],
        near_rows, far_rows, own, front_sums, back_sums,
    )
    hall = trade(load, "real")
    grad_part = pair_sums(
        hall, near_rows, far_rows, front, real_rows, front_sq, back_sq, total_flows, total_real, 256
    )
    (grad_own,) = call_once(sum_kernel, [grad_part.shape], trade(grad_part, "real"))
    part = back_steps(trade(grad_own, "real"), val, sig, hidden)
    grad = swap_sum(part, "gen", gen_count, ((1,), (2,), (4, 8, 12)))
    (square,) = call_once(square_kernel, [(real_count, 8, 128)], grad)
    update, loss = pl.pallas_call(
        scale_kernel,
        grid=(1,),
        out_shape=[
            jax.ShapeDtypeStruct((local_steps, width), f32),
            jax.ShapeDtypeStruct((1,), f32),
        ],
        in_specs=[fixed(grad.shape), fixed(square.shape)],
        out_specs=[fixed((local_steps, width)), pl.BlockSpec(memory_space=SMEM)],
        compiler_params=params(),
    )(grad, trade(square, "real"))
    return (update.T, loss.reshape(()))


def solution(mesh):
    in_specs = (P("gen", None), P(None, "real"), P("gen"), P("real", None))
    out_specs = (P(None, "real"), P())
    body = functools.partial(per_device, mesh.shape["real"], mesh.shape["gen"])
    return jax.shard_map(
        body, mesh=mesh, in_specs=in_specs, out_specs=out_specs, check_vma=False
    )
```
